32 devices in a mesh: groups: 2 (over y), rows: 4 (over z), cols: 4 (over x, core).
Axes of the slice: x: 2, y: 2, z: 4, core: 2. Of those that a mesh axis runs over, the one named last changes fastest.
Arguments:
- inputs: bfloat16 [32, 6144], P(None, ('groups', 'rows', 'cols')), parts along dimension 1, may hold values from -6 to 6
- task_ids: int32 [6144], P(('groups', 'rows', 'cols')), parts along dimension 0, may hold values from 0 to 2999
- scale_table: float32 [3000], replicated, may hold values from 0.5 to 2
- probes: float32 [16, 6144], P(None, ('groups', 'rows', 'cols')), parts along dimension 1, may hold values from -6 to 6
- solves: float32 [16, 6144], P(None, ('groups', 'rows', 'cols')), parts along dimension 1, may hold values from -6 to 6
- alpha_solve: float32 [6144], P(('groups', 'rows', 'cols')), parts along dimension 0, may hold values from -6 to 6
- w_in: bfloat16 [32, 256], replicated, may hold values from -1 to 1
- b_in: float32 [256], replicated, may hold values from -3 to 3
- w_out: bfloat16 [256, 64], replicated, may hold values from -0.375 to 0.375
Outputs:
- feat_grad: float32 [64, 6144], P(None, ('groups', 'rows', 'cols')), parts along dimension 1
- grad_w_in: float32 [64, 256], P('groups'), parts along dimension 0
- grad_b_in: float32 [512], P('groups'), parts along dimension 0
- grad_w_out: float32 [512, 64], P('groups'), parts along dimension 0
The draws below stay inside these ranges and needn't reach their ends.
There are 2 independent parts, one for each index of `groups`. The reference program is written for one: setup_inputs(seed, part) draws one part's arguments, and reference() takes and returns one part's arrays. A program takes and returns all parts, laid end to end along the dimension named above; an argument that names none is the same for every part. Nothing has to cross between parts.
All inputs are finite; a program needn't handle non-finite values.
Results may differ from the reference program's by a relative error of at most 0.0098.
Values may be sent and summed in bfloat16 or wider, within the bound.
A program may use at most 64 MiB of HBM per device.

```python
import math
import jax
import jax.numpy as jnp
from jax import lax

IN = 32
H = 256
F = 64
TASKS = 3000
PROBES = 16
TR_DEV = 192
TRIALS = 3072
N_ROWS = 4
N_COLS = 4


def set_ends(array, key, smallest, top_value):
    longest = array.shape.index(max(array.shape))
    spots = []
    for shift in (0, 1):
        where = [jax.random.randint(jax.random.fold_in(key, axis), (), 0, length) for axis, length in enumerate(array.shape)]
        where[longest] = (where[longest] + shift) % array.shape[longest]
        spots.append(tuple(where))
    return array.at[spots[0]].set(smallest).at[spots[1]].set(top_value)


def shard_levels(own_key, dims, split, smallest, top_value):
    factor_of, own = 1.0, jax.random.fold_in(own_key, 6)
    for position, parts in split:
        draws = jnp.exp(jax.random.uniform(jax.random.fold_in(own, position), (parts,), jnp.float32, smallest / len(split), top_value / len(split)))
        factor_of = factor_of * jnp.repeat(draws, dims[position] // parts).reshape([-1 if axis == position else 1 for axis in range(len(dims))])
    return factor_of


def normal_values(rng, shape, spread, most, shards=(), dtype=jnp.bfloat16):
    factor_of = shard_levels(rng, shape, shards, -0.22, 0.18) if shards else 1.0
    result = jax.random.normal(rng, shape, jnp.float32) * spread * factor_of
    return jnp.minimum(jnp.maximum(result, -most), most).astype(dtype)


def setup_inputs(seed: int = 0, part: int = 0) -> dict:
    arg_keys = jax.random.split(jax.random.key(seed), 10)
    part_keys = jax.random.split(jax.random.fold_in(arg_keys[9], part), 10)
    inputs = normal_values(part_keys[0], (IN, TRIALS), 1.0, 6.0, ((1, 16),))
    task_ids = set_ends(jax.random.randint(part_keys[1], (TRIALS,), 0, TASKS), jax.random.fold_in(part_keys[1], 1), 0, TASKS - 1).astype(jnp.int32)
    scale_table = jnp.clip(jnp.exp(jax.random.uniform(arg_keys[2], (TASKS,), jnp.float32, math.log(0.5), math.log(2.0))), 0.5, 2.0)
    probes = normal_values(part_keys[3], (PROBES, TRIALS), 1.0, 6.0, ((1, 16),), jnp.float32)
    solves = normal_values(part_keys[4], (PROBES, TRIALS), 1.0, 6.0, ((1, 16),), jnp.float32)
    alpha_solve = normal_values(part_keys[5], (TRIALS,), 1.0, 6.0, ((0, 16),), jnp.float32)
    w_in = normal_values(arg_keys[6], (IN, H), IN ** -0.5, 1.0)
    b_in = normal_values(arg_keys[7], (H,), 0.5, 3.0, (), jnp.float32)
    w_out = normal_values(arg_keys[8], (H, F), H ** -0.5, 0.375)
    return dict(inputs=inputs, task_ids=task_ids, scale_table=scale_table, probes=probes, solves=solves, alpha_solve=alpha_solve, w_in=w_in, b_in=b_in, w_out=w_out)


kernel_rate = 1.0

def project(inputs, w_in, b_in, w_out):
    preact = lax.dot_general(w_in, inputs, (((0,), (0,)), ((), ())), preferred_element_type=jnp.float32) + b_in[:, None]
    hidden = jax.nn.silu(preact).astype(jnp.bfloat16)
    feat_rows = lax.dot_general(w_out, hidden, (((0,), (0,)), ((), ())), preferred_element_type=jnp.float32).astype(jnp.bfloat16)
    return (preact, hidden, feat_rows)

def tile_terms(row_feats, row_vecs, col_feats, col_vecs):
    probe_count = (row_vecs.shape[0] - 1) // 2
    feat_width = row_feats.shape[0]
    row_float = row_feats.astype(jnp.float32)
    col_float = col_feats.astype(jnp.float32)
    row_norm = lax.optimization_barrier(jnp.sum(row_float * row_float, 0))
    col_norm = lax.optimization_barrier(jnp.sum(col_float * col_float, 0))
    inner_prod = lax.dot_general(row_feats, col_feats, (((0,), (0,)), ((), ())), preferred_element_type=jnp.float32)
    kernel = jnp.exp(-(row_norm[:, None] + col_norm[None, :] - 2.0 * inner_prod) * (kernel_rate / feat_width))
    swapped = jnp.concatenate([col_vecs[probe_count:2 * probe_count], col_vecs[:probe_count]], 0)
    pair_term = lax.dot_general(row_vecs[:2 * probe_count], swapped, (((0,), (0,)), ((), ())), preferred_element_type=jnp.float32) / (2.0 * probe_count)
    pair_term = pair_term - row_vecs[2 * probe_count].astype(jnp.float32)[:, None] * col_vecs[2 * probe_count].astype(jnp.float32)[None, :]
    weight = pair_term * kernel
    weight_sum = lax.optimization_barrier(jnp.sum(weight, 1))
    totals = lax.dot_general(col_feats, weight.astype(jnp.bfloat16), (((1,), (1,)), ((), ())), preferred_element_type=jnp.float32)
    return (totals, weight_sum)

def backward(inputs, preact, hidden, feat_grad, w_out):
    grad_feats = feat_grad.astype(jnp.bfloat16)
    grad_hidden = jnp.dot(w_out, grad_feats, preferred_element_type=jnp.float32)
    sigmoid_pre = jax.nn.sigmoid(preact)
    grad_pre = grad_hidden * (sigmoid_pre * (1.0 + preact * (1.0 - sigmoid_pre)))
    grad_pre_b = grad_pre.astype(jnp.bfloat16)
    grad_w_in = lax.dot_general(inputs, grad_pre_b, (((1,), (1,)), ((), ())), preferred_element_type=jnp.float32)
    grad_b_in = lax.optimization_barrier(jnp.sum(grad_pre, 1))
    grad_w_out = lax.dot_general(hidden, grad_feats, (((1,), (1,)), ((), ())), preferred_element_type=jnp.float32)
    return (grad_w_in, grad_b_in, grad_w_out)

def reference(inputs, task_ids, scale_table, probes, solves, alpha_solve, w_in, b_in, w_out):
    preact, hidden, feat_rows = project(inputs, w_in, b_in, w_out)
    trial_scale = jnp.take(scale_table, task_ids)
    scaled_vecs = (jnp.concatenate([solves, probes, alpha_solve[None, :]], 0) * trial_scale[None, :]).astype(jnp.bfloat16)
    feat_width = feat_rows.shape[0]
    block_rows = TR_DEV * N_COLS

    def one_block(first_row):
        row_feats = lax.dynamic_slice_in_dim(feat_rows, first_row, block_rows, 1)
        row_vecs = lax.dynamic_slice_in_dim(scaled_vecs, first_row, block_rows, 1)
        totals, weight_sum = tile_terms(row_feats, row_vecs, feat_rows, scaled_vecs)
        return (totals - weight_sum[None, :] * row_feats.astype(jnp.float32)) * (2.0 * kernel_rate / feat_width)
    firsts = (jnp.arange(N_ROWS) * block_rows).astype(jnp.int32)
    blocks = lax.map(one_block, firsts)
    feat_grad = jnp.transpose(blocks, (1, 0, 2)).reshape(feat_width, TRIALS)
    grad_w_in, grad_b_in, grad_w_out = backward(inputs, preact, hidden, feat_grad, w_out)
    factor = 1.0 / math.sqrt(TRIALS)
    return (feat_grad, grad_w_in * factor, grad_b_in * factor, grad_w_out * factor)
```

```python
import functools
import math

import jax
import jax.numpy as jnp
from jax import lax
from jax.experimental import pallas as pl
from jax.experimental.pallas import tpu as pltpu
from jax.sharding import PartitionSpec as P

kernel_rate = 1.0
MESH = pl.DeviceIdType.MESH
LANES = 128


def split3(value):
    high = value.astype(jnp.bfloat16).astype(jnp.float32)
    rest = value - high
    mid = rest.astype(jnp.bfloat16).astype(jnp.float32)
    low = (rest - mid).astype(jnp.bfloat16).astype(jnp.float32)
    return high, mid, low


def whole_kernel(
    R, C,
    inputs_ref, ids_ref, table_ref, probes_ref, solves_ref, alpha_ref, w_in_ref, b_in_ref, w_out_ref,
    fgrad_ref, gw_in_ref, gb_in_ref, gw_out_ref,
    buf, parts, rs_buf, ag_buf, ag_size,
    recv_sem, send_sem, rs_send, rs_recv, ag_send, ag_recv,
):
    n = R * C
    r, c = lax.axis_index("rows"), lax.axis_index("cols")
    me = r * C + c
    trials = inputs_ref.shape[1]
    feat_width = w_out_ref.shape[1]
    probe_count = probes_ref.shape[0]
    pieces = parts.shape[0]

    def coords(q):
        return {"rows": q // C, "cols": lax.rem(q, C)}

    def other(k):
        return lax.rem(me + k, n)

    barrier = pltpu.get_barrier_semaphore()

    @pl.loop(1, n)
    def _(k):
        pl.semaphore_signal(barrier, inc=1, device_id=coords(other(k)), device_id_type=MESH)

    inputs = inputs_ref[...]
    preact = lax.dot_general(
        inputs, w_in_ref[...], (((0,), (0,)), ((), ())), preferred_element_type=jnp.float32
    ) + b_in_ref[...]
    sig = 1.0 / (1.0 + jnp.exp(-preact))
    hidden = (preact * sig).astype(jnp.bfloat16)
    feats = jnp.dot(hidden, w_out_ref[...], preferred_element_type=jnp.float32).astype(jnp.bfloat16)
    feats_f = feats.astype(jnp.float32)
    sqnorm = jnp.sum(feats_f * feats_f, 1, keepdims=True)

    ids = ids_ref[...]
    lo, hi = lax.rem(ids, LANES), ids // LANES
    table = table_ref[...]
    groups = table.shape[0]
    hot = (lax.broadcasted_iota(jnp.int32, (LANES, trials), 0) == lo).astype(jnp.float32).astype(jnp.bfloat16)
    terms = jnp.concatenate(split3(table), 0).astype(jnp.bfloat16)
    found = jnp.dot(terms, hot, preferred_element_type=jnp.float32)
    found = found[:groups] + found[groups : 2 * groups] + found[2 * groups :]
    mine = lax.broadcasted_iota(jnp.int32, (groups, trials), 0) == hi
    scale = jnp.sum(jnp.where(mine, found, 0.0), 0, keepdims=True)

    vec_rows = LANES - feat_width
    vecs = jnp.concatenate(
        [
            solves_ref[...] * scale,
            probes_ref[...] * scale,
            jnp.broadcast_to(alpha_ref[...] * scale, (vec_rows - 2 * probe_count, trials)),
        ],
        0,
    )
    pad = -trials % LANES
    vecs = jnp.concatenate([vecs, jnp.zeros((vec_rows, pad), jnp.float32)], 1)
    vecs = jnp.transpose(vecs)[:trials].astype(jnp.bfloat16).astype(jnp.float32)

    first_u, first_z = feat_width, feat_width + probe_count
    at_a = feat_width + 2 * probe_count
    lane = lax.broadcasted_iota(jnp.int32, (trials, LANES), 1)
    n_hi, n_mid, n_lo = split3(sqnorm)
    base = jnp.concatenate([feats_f, vecs], 1)
    payload = jnp.where(
        lane <= at_a,
        base,
        jnp.where(
            lane == at_a + 1, n_hi,
            jnp.where(
                lane == at_a + 2, n_mid,
                jnp.where(lane == at_a + 3, n_lo, jnp.where(lane <= at_a + 6, 1.0, 0.0)),
            ),
        ),
    )
    buf[c * R + r] = payload.astype(jnp.bfloat16)

    rate = kernel_rate / feat_width
    row_exp = jnp.where(
        lane < feat_width,
        base * (2.0 * rate),
        jnp.where(
            lane <= at_a, 0.0,
            jnp.where(
                lane <= at_a + 3, -rate,
                jnp.where(
                    lane == at_a + 4, n_hi * -rate,
                    jnp.where(
                        lane == at_a + 5, n_mid * -rate,
                        jnp.where(lane == at_a + 6, n_lo * -rate, 0.0),
                    ),
                ),
            ),
        ),
    )
    swapped = jnp.concatenate(
        [feats_f, vecs[:, probe_count : 2 * probe_count], vecs[:, :probe_count], vecs[:, 2 * probe_count :]], 1
    )
    row_pair = jnp.where(
        lane < feat_width, 0.0,
        jnp.where(lane < at_a, swapped * (0.5 / probe_count), jnp.where(lane == at_a, -swapped, 0.0)),
    )
    left = jnp.concatenate([row_exp, row_pair], 0).astype(jnp.bfloat16)

    pl.semaphore_wait(barrier, n - 1)

    def copy(slot, device):
        return pltpu.make_async_remote_copy(
            src_ref=buf.at[slot], dst_ref=buf.at[slot], send_sem=send_sem, recv_sem=recv_sem.at[slot],
            device_id=device, device_id_type=MESH,
        )

    def wait_slot(slot):
        pltpu.make_async_copy(buf.at[slot], buf.at[slot], recv_sem.at[slot]).wait()

    bits = []
    while (1 << len(bits)) < C:
        bits.insert(0, 1 << len(bits))

    def forward(mask, slot):
        for bit in bits:
            if mask == 0 or bit < (mask & -mask):
                copy(slot, {"rows": r, "cols": c ^ bit}).start()

    def compute(mask, carry):
        group = c ^ mask

        def pair_step(step, carry):
            total, sums = carry
            cols = buf[pl.ds(group * R + 2 * step, 2)].reshape(2 * trials, LANES)
            both = lax.dot_general(left, cols, (((1,), (1,)), ((), ())), preferred_element_type=jnp.float32)
            weight = both[trials:] * jnp.exp(both[:trials])
            for k in range(2 * trials // LANES):
                sums = sums + weight[:, k * LANES : (k + 1) * LANES]
            total = total + jnp.dot(weight.astype(jnp.bfloat16), cols, preferred_element_type=jnp.float32)
            return total, sums

        return lax.fori_loop(0, R // 2, pair_step, carry)

    own = c * R + r

    @pl.loop(1, R)
    def _(k):
        copy(own, {"rows": lax.rem(r + k, R), "cols": c}).start()

    forward(0, own)

    @pl.loop(1, R)
    def _(k):
        slot = c * R + lax.rem(r + k, R)
        wait_slot(slot)
        forward(0, slot)

    empty = jnp.zeros((trials, LANES), jnp.float32)
    carry = compute(0, (empty, empty))
    masks = sorted(range(1, C), key=lambda m: (-(m & -m), m))
    for mask in masks:
        @pl.loop(0, R)
        def _(k):
            slot = (c ^ mask) * R + lax.rem(r + k, R)
            wait_slot(slot)
            forward(mask, slot)

        carry = compute(mask, carry)
    total, sums = carry

    weight_sum = jnp.sum(sums, 1, keepdims=True)
    feat_grad = (total[:, :feat_width] - weight_sum * feats_f) * (2.0 * rate)
    grad_feats = feat_grad.astype(jnp.bfloat16)
    grad_hidden = lax.dot_general(
        grad_feats, w_out_ref[...], (((1,), (1,)), ((), ())), preferred_element_type=jnp.float32
    )
    grad_pre = grad_hidden * (sig * (1.0 + preact * (1.0 - sig)))
    g_in = jnp.dot(inputs, grad_pre.astype(jnp.bfloat16), preferred_element_type=jnp.float32)
    g_out = lax.dot_general(
        grad_feats, hidden, (((0,), (0,)), ((), ())), preferred_element_type=jnp.float32
    )
    g_bias = jnp.broadcast_to(jnp.sum(grad_pre, 0, keepdims=True), (8, grad_pre.shape[1]))
    packed = jnp.concatenate([g_in, g_out, g_bias], 0)
    for p in range(pieces):
        for h in range(2):
            parts[p, 8 * h : 8 * h + 8] = packed[8 * p : 8 * p + 8, h * LANES : (h + 1) * LANES]

    def piece_copy(p):
        return pltpu.make_async_remote_copy(
            src_ref=parts.at[p], dst_ref=rs_buf.at[me], send_sem=rs_send.at[p], recv_sem=rs_recv,
            device_id=coords(p), device_id_type=MESH,
        )

    @pl.loop(0, pieces)
    def _(k):
        p = lax.rem(me + k, pieces)

        @pl.when(p != me)
        def _():
            piece_copy(p).start()

    wide = jnp.concatenate([feat_grad, jnp.zeros((trials, LANES - feat_width), jnp.float32)], 1)
    wide = jnp.concatenate([wide, jnp.zeros((pad, LANES), jnp.float32)], 0)
    fgrad_ref[...] = jnp.transpose(wide)[:feat_width, :trials]

    def ag_copy(k):
        return pltpu.make_async_remote_copy(
            src_ref=ag_buf.at[me], dst_ref=ag_buf.at[me], send_sem=ag_send, recv_sem=ag_recv,
            device_id=coords(other(k)), device_id_type=MESH,
        )

    factor = 1.0 / math.sqrt(trials * n)

    @pl.when(me < pieces)
    def _():
        rs_buf[me] = parts[me]
        pltpu.make_async_copy(rs_buf.at[pl.ds(0, n - 1)], rs_buf.at[pl.ds(0, n - 1)], rs_recv).wait()
        summed = jnp.sum(rs_buf[...], 0) * factor
        ag_buf[me] = summed.astype(jnp.bfloat16)

        @pl.loop(1, n)
        def _(k):
            ag_copy(k).start()

        view = ag_buf.at[pl.ds(0, pieces - 1)]
        pltpu.make_async_copy(view, view, ag_recv).wait()

    @pl.when(me >= pieces)
    def _():
        pltpu.make_async_copy(ag_buf, ag_buf, ag_recv).wait()

    def unpack(first, count):
        rows = []
        for p in range(first, first + count):
            piece = ag_buf[p].astype(jnp.float32)
            rows.append(jnp.concatenate([piece[:8], piece[8:]], 1))
        return jnp.concatenate(rows, 0) if count > 1 else rows[0]

    in_pieces, out_pieces = g_in.shape[0] // 8, feat_width // 8
    gw_in_ref[...] = unpack(0, in_pieces)
    gw_out_ref[...] = unpack(in_pieces, out_pieces)
    gb_in_ref[...] = unpack(in_pieces + out_pieces, 1)[:1]

    pltpu.make_async_copy(buf.at[pl.ds(0, n - 1)], buf.at[pl.ds(0, n - 1)], send_sem).wait()

    @pl.loop(0, pieces)
    def _(p):
        @pl.when(p != me)
        def _():
            piece_copy(p).wait_send()

    @pl.when(me < pieces)
    def _():
        pltpu.make_async_copy(ag_size, ag_size, ag_send).wait()


def solution(mesh):
    R, C = mesh.shape["rows"], mesh.shape["cols"]
    n = R * C

    def body(inputs, task_ids, scale_table, probes, solves, alpha_solve, w_in, b_in, w_out):
        width, trials = inputs.shape
        hidden_width, feat_width = w_out.shape
        pieces = (width + feat_width) // 8 + 1
        tasks = scale_table.shape[0]
        table = jnp.pad(scale_table, (0, -tasks % (8 * LANES))).reshape(-1, LANES)
        vmem = pl.BlockSpec(memory_space=pltpu.VMEM)
        fgrad, gw_in, gb_in, gw_out = pl.pallas_call(
            functools.partial(whole_kernel, R, C),
            out_shape=(
                jax.ShapeDtypeStruct((feat_width, trials), jnp.float32),
                jax.ShapeDtypeStruct((width, hidden_width), jnp.float32),
                jax.ShapeDtypeStruct((1, hidden_width), jnp.float32),
                jax.ShapeDtypeStruct((feat_width, hidden_width), jnp.float32),
            ),
            in_specs=[vmem] * 9,
            out_specs=(vmem,) * 4,
            scratch_shapes=[
                pltpu.VMEM((n, trials, LANES), jnp.bfloat16),
                pltpu.VMEM((pieces, 16, LANES), jnp.float32),
                pltpu.VMEM((n, 16, LANES), jnp.float32),
                pltpu.VMEM((pieces, 16, LANES), jnp.bfloat16),
                pltpu.VMEM((n - 1, 16, LANES), jnp.bfloat16),
                pltpu.SemaphoreType.DMA((n,)),
                pltpu.SemaphoreType.DMA,
                pltpu.SemaphoreType.DMA((pieces,)),
                pltpu.SemaphoreType.DMA,
                pltpu.SemaphoreType.DMA,
                pltpu.SemaphoreType.DMA,
            ],
            compiler_params=pltpu.CompilerParams(
                collective_id=0, has_side_effects=True, vmem_limit_bytes=48 * 1024 * 1024
            ),
        )(
            inputs, task_ids[None, :], table, probes, solves, alpha_solve[None, :], w_in, b_in[None, :], w_out
        )
        return fgrad, gw_in, gb_in[0], jnp.transpose(gw_out)

    split = ("groups", "rows", "cols")
    return jax.shard_map(
        body,
        mesh=mesh,
        in_specs=(
            P(None, split), P(split), P(), P(None, split), P(None, split), P(split), P(), P(), P(),
        ),
        out_specs=(P(None, split), P("groups", None), P("groups"), P("groups", None)),
        check_vma=False,
    )
```

```python
import functools
import math

import jax
import jax.numpy as jnp
from jax import lax
from jax.experimental import pallas as pl
from jax.experimental.pallas import tpu as pltpu
from jax.sharding import PartitionSpec as P

kernel_rate = 1.0
MESH = pl.DeviceIdType.MESH
LANES = 128


def split3(value):
    high = value.astype(jnp.bfloat16).astype(jnp.float32)
    rest = value - high
    mid = rest.astype(jnp.bfloat16).astype(jnp.float32)
    low = (rest - mid).astype(jnp.bfloat16).astype(jnp.float32)
    return high, mid, low


def whole_kernel(
    R, C,
    *refs_and_scratch,
):
    operands, refs = refs_and_scratch[:9], refs_and_scratch[9:]
    fgrad_ref, sums_ref, *refs = refs
    staged, (load_sem, *refs) = refs[:9], refs[9:]
    inputs_ref, ids_ref, table_ref, probes_ref, solves_ref, alpha_ref, w_in_ref, b_in_ref, w_out_t_ref = staged
    (
        buf, left_buf, swap, parts, rs_buf, ag_buf, ag_size,
        recv_sem, send_sem, core_send, core_recv, rs_send, rs_recv, ag_send, ag_recv,
    ) = refs
    n = R * C
    r, c = lax.axis_index("rows"), lax.axis_index("cols")
    me = r * C + c
    trials = inputs_ref.shape[1]
    feat_width = w_out_t_ref.shape[0]
    probe_count = probes_ref.shape[0]
    pieces = parts.shape[0]

    def coords(q):
        return {"rows": q // C, "cols": lax.rem(q, C)}

    def other(k):
        return lax.rem(me + k, n)

    barrier = pltpu.get_barrier_semaphore()

    @pl.loop(1, n)
    def _(k):
        pl.semaphore_signal(barrier, inc=1, device_id=coords(other(k)), device_id_type=MESH)

    loads = [
        pltpu.make_async_copy(operands[k], staged[k], load_sem.at[k]) for k in range(9)
    ]
    for load in loads:
        load.start()

    for load in loads:
        load.wait()

    ids = ids_ref[...]
    lo, hi = lax.rem(ids, LANES), ids // LANES
    flat = table_ref[...]
    tasks = flat.shape[1]
    groups = -(-tasks // (8 * LANES)) * 8
    flat = jnp.concatenate([flat, jnp.zeros((1, groups * LANES - tasks), jnp.float32)], 1)
    table = jnp.concatenate([flat[:, k * LANES : (k + 1) * LANES] for k in range(groups)], 0)
    hot = (lax.broadcasted_iota(jnp.int32, (LANES, trials), 0) == lo).astype(jnp.float32).astype(jnp.bfloat16)
    terms = jnp.concatenate(split3(table), 0).astype(jnp.bfloat16)
    found = jnp.dot(terms, hot, preferred_element_type=jnp.float32)
    found = found[:groups] + found[groups : 2 * groups] + found[2 * groups :]
    mine = lax.broadcasted_iota(jnp.int32, (groups, trials), 0) == hi
    scale = jnp.sum(jnp.where(mine, found, 0.0), 0, keepdims=True)

    inputs = inputs_ref[...]
    width, half = inputs.shape[0], trials // 2
    raw_lanes = width + 2 * probe_count
    pad = -trials % LANES
    raw = jnp.concatenate(
        [
            inputs.astype(jnp.float32),
            solves_ref[...] * scale,
            probes_ref[...] * scale,
            jnp.broadcast_to(alpha_ref[...] * scale, (LANES - raw_lanes, trials)),
        ],
        0,
    )
    raw = jnp.transpose(jnp.concatenate([raw, jnp.zeros((LANES, pad), jnp.float32)], 1))[:trials]
    raw = raw.astype(jnp.bfloat16).astype(jnp.float32)

    chips = n // 2
    here, side = r * (C // 2) + c // 2, lax.rem(c, 2)
    main_part = jnp.concatenate([raw[:half, :raw_lanes], raw[half:, :raw_lanes]], 1)
    tile_lane = lax.broadcasted_iota(jnp.int32, (16, LANES), 1)
    a_part = jnp.zeros((16, LANES), jnp.float32)
    for k in range(trials // 16):
        a_part = jnp.where(tile_lane == k, raw[16 * k : 16 * k + 16, raw_lanes : raw_lanes + 1], a_part)
    buf[here, :half] = main_part.astype(jnp.bfloat16)
    buf[here, half:] = a_part.astype(jnp.bfloat16)

    pl.semaphore_wait(barrier, n - 1)

    def send(k):
        chip = here ^ k
        pltpu.make_async_remote_copy(
            src_ref=buf.at[here], dst_ref=buf.at[here], send_sem=send_sem, recv_sem=recv_sem.at[here],
            device_id={"rows": chip // (C // 2), "cols": lax.rem(chip, C // 2) * 2 + side},
            device_id_type=MESH,
        ).start()

    far = chips // 2

    @pl.loop(far, chips)
    def _(k):
        send(k)

    @pl.loop(1, far)
    def _(k):
        send(k)

    w_in, b_in = w_in_ref[...], b_in_ref[...]
    hidden_width = w_in.shape[1]
    preact = lax.dot_general(
        inputs, w_in, (((0,), (0,)), ((), ())), preferred_element_type=jnp.float32
    ) + b_in
    sig = 1.0 / (1.0 + jnp.exp(-preact))
    hidden = (preact * sig).astype(jnp.bfloat16)
    w_out_t = w_out_t_ref[...]
    feats = lax.dot_general(
        hidden, w_out_t, (((1,), (1,)), ((), ())), preferred_element_type=jnp.float32
    ).astype(jnp.bfloat16)
    feats_f = feats.astype(jnp.float32)
    sqnorm = jnp.sum(feats_f * feats_f, 1, keepdims=True)
    vecs = raw[:, width : width + LANES - feat_width]

    first_u, first_z = feat_width, feat_width + probe_count
    at_a = feat_width + 2 * probe_count
    lane = lax.broadcasted_iota(jnp.int32, (trials, LANES), 1)
    n_hi, n_mid, n_lo = split3(sqnorm)
    base = jnp.concatenate([feats_f, vecs], 1)
    rate = kernel_rate / feat_width
    row_exp = jnp.where(
        lane < feat_width,
        base * (2.0 * rate),
        jnp.where(
            lane <= at_a, 0.0,
            jnp.where(
                lane <= at_a + 3, -rate,
                jnp.where(
                    lane == at_a + 4, n_hi * -rate,
                    jnp.where(
                        lane == at_a + 5, n_mid * -rate,
                        jnp.where(lane == at_a + 6, n_lo * -rate, 0.0),
                    ),
                ),
            ),
        ),
    )
    swapped = jnp.concatenate(
        [feats_f, vecs[:, probe_count : 2 * probe_count], vecs[:, :probe_count], vecs[:, 2 * probe_count :]], 1
    )
    row_pair = jnp.where(
        lane < feat_width, 0.0,
        jnp.where(lane < at_a, swapped * (0.5 / probe_count), jnp.where(lane == at_a, -swapped, 0.0)),
    )
    left_buf[0, 0] = row_exp.astype(jnp.bfloat16)
    left_buf[0, 1] = row_pair.astype(jnp.bfloat16)

    def core_copy(refs, which):
        return pltpu.make_async_remote_copy(
            src_ref=refs.at[0], dst_ref=refs.at[1], send_sem=core_send.at[which], recv_sem=core_recv.at[which],
            device_id={"rows": r, "cols": c ^ 1}, device_id_type=MESH,
        )

    def wait_chip(k):
        chip = here ^ k
        pltpu.make_async_copy(buf.at[chip], buf.at[chip], recv_sem.at[chip]).wait()

    core_copy(left_buf, 0).start()
    core_copy(left_buf, 0).wait()
    left = jnp.concatenate([left_buf[0, 0], left_buf[1, 0], left_buf[0, 1], left_buf[1, 1]], 0)

    blank = jnp.zeros((width, hidden_width), jnp.bfloat16)
    gap = jnp.zeros((2 * probe_count, 2 * hidden_width), jnp.bfloat16)
    first_layer = jnp.concatenate(
        [
            jnp.concatenate([w_in, blank], 1),
            gap,
            jnp.concatenate([blank, w_in], 1),
            gap,
        ],
        0,
    )
    bias = jnp.concatenate([b_in, b_in], 1)
    second_layer = jnp.concatenate([w_out_t, jnp.zeros((LANES - feat_width, hidden_width), jnp.bfloat16)], 0)
    s_row = lax.broadcasted_iota(jnp.int32, (2 * LANES, LANES), 0)
    s_lane = lax.broadcasted_iota(jnp.int32, (2 * LANES, LANES), 1)
    lane2 = lax.broadcasted_iota(jnp.int32, (trials, LANES), 1)
    block = lax.rem(lax.broadcasted_iota(jnp.int32, (trials, LANES), 0), half) // 16
    places, a_masks = [], []
    for h in range(2):
        vec_place = (s_row == s_lane - feat_width + width + h * raw_lanes) & (s_lane >= feat_width) & (s_lane < at_a)
        place = vec_place | ((s_row >= LANES) & (s_lane == at_a))
        places.append(place.astype(jnp.float32).astype(jnp.bfloat16))
        a_masks.append((lane2 == block + h * (half // 16)).astype(jnp.float32).astype(jnp.bfloat16))

    def columns(pair):
        blocks = buf[pl.ds(2 * pair, 2)]
        main = blocks[:, :half].reshape(trials, LANES)
        tiles = jnp.concatenate([blocks[0, half:]] * (half // 16) + [blocks[1, half:]] * (half // 16), 0)
        pre = jnp.dot(main, first_layer, preferred_element_type=jnp.float32) + bias
        hid = (pre * (1.0 / (1.0 + jnp.exp(-pre)))).astype(jnp.bfloat16)
        found = []
        for h in range(2):
            value = lax.dot_general(
                hid[:, h * hidden_width : (h + 1) * hidden_width], second_layer,
                (((1,), (1,)), ((), ())), preferred_element_type=jnp.float32,
            ) + jnp.dot(
                jnp.concatenate([main, tiles * a_masks[h]], 1), places[h], preferred_element_type=jnp.float32
            )
            value = value.astype(jnp.bfloat16).astype(jnp.float32)
            norm = jnp.sum(jnp.where(lane2 < feat_width, value * value, 0.0), 1, keepdims=True)
            high, mid, low = split3(norm)
            found.append(
                jnp.where(
                    lane2 <= at_a, value,
                    jnp.where(
                        lane2 == at_a + 1, high,
                        jnp.where(
                            lane2 == at_a + 2, mid,
                            jnp.where(lane2 == at_a + 3, low, jnp.where(lane2 <= at_a + 6, 1.0, 0.0)),
                        ),
                    ),
                )
            )
        return jnp.concatenate(found, 0).astype(jnp.bfloat16)

    def add_pair(p, carry):
        total, sums = carry
        cols = columns((here // 2) ^ p)
        both = lax.dot_general(left, cols, (((1,), (1,)), ((), ())), preferred_element_type=jnp.float32)
        weight = both[2 * trials :] * jnp.exp(both[: 2 * trials])
        for j in range(2 * trials // LANES):
            sums = sums + weight[:, j * LANES : (j + 1) * LANES]
        total = total + jnp.dot(weight.astype(jnp.bfloat16), cols, preferred_element_type=jnp.float32)
        return total, sums

    def step(p, carry):
        wait_chip(2 * p)
        wait_chip(2 * p + 1)
        return add_pair(p, carry)

    empty = jnp.zeros((2 * trials, LANES), jnp.float32)
    wait_chip(1)
    carry = add_pair(0, (empty, empty))
    total, sums = lax.fori_loop(1, chips // 2, step, carry)

    weight_sum = jnp.sum(sums, 1, keepdims=True)
    lane4 = lax.broadcasted_iota(jnp.int32, (2 * trials, LANES), 1)
    mixed = jnp.where(lane4 < feat_width, total, weight_sum)
    swap[0] = mixed[trials:]
    core_copy(swap, 1).start()
    core_copy(swap, 1).wait()
    mixed = mixed[:trials] + swap[1]
    total, weight_sum = mixed[:, :feat_width], mixed[:, feat_width : feat_width + 1]
    feat_grad = (total - weight_sum * feats_f) * (2.0 * rate)
    grad_feats = feat_grad.astype(jnp.bfloat16)
    grad_hidden = jnp.dot(grad_feats, w_out_t, preferred_element_type=jnp.float32)
    grad_pre = grad_hidden * (sig * (1.0 + preact * (1.0 - sig)))
    g_in = jnp.dot(inputs, grad_pre.astype(jnp.bfloat16), preferred_element_type=jnp.float32)
    g_out = lax.dot_general(
        grad_feats, hidden, (((0,), (0,)), ((), ())), preferred_element_type=jnp.float32
    )
    g_bias = jnp.broadcast_to(jnp.sum(grad_pre, 0, keepdims=True), (8, grad_pre.shape[1]))
    packed = jnp.concatenate([g_in, g_out, g_bias], 0)
    for p in range(pieces):
        for h in range(2):
            parts[p, 8 * h : 8 * h + 8] = packed[8 * p : 8 * p + 8, h * LANES : (h + 1) * LANES]

    def piece_copy(p):
        return pltpu.make_async_remote_copy(
            src_ref=parts.at[p], dst_ref=rs_buf.at[me], send_sem=rs_send.at[p], recv_sem=rs_recv,
            device_id=coords(p), device_id_type=MESH,
        )

    @pl.loop(0, pieces)
    def _(k):
        p = lax.rem(me + k, pieces)

        @pl.when(p != me)
        def _():
            piece_copy(p).start()

    wide = jnp.concatenate([feat_grad, jnp.zeros((trials, LANES - feat_width), jnp.float32)], 1)
    wide = jnp.concatenate([wide, jnp.zeros((pad, LANES), jnp.float32)], 0)
    fgrad_ref[...] = jnp.transpose(wide)[:feat_width, :trials]

    def ag_copy(k):
        return pltpu.make_async_remote_copy(
            src_ref=ag_buf.at[me], dst_ref=ag_buf.at[me], send_sem=ag_send, recv_sem=ag_recv,
            device_id=coords(other(k)), device_id_type=MESH,
        )

    factor = 1.0 / math.sqrt(trials * n)

    @pl.when(me < pieces)
    def _():
        rs_buf[me] = parts[me]
        pltpu.make_async_copy(rs_buf.at[pl.ds(0, n - 1)], rs_buf.at[pl.ds(0, n - 1)], rs_recv).wait()
        summed = jnp.sum(rs_buf[...], 0) * factor
        ag_buf[me] = summed.astype(jnp.bfloat16)

        @pl.loop(1, n)
        def _(k):
            ag_copy(k).start()

        view = ag_buf.at[pl.ds(0, pieces - 1)]
        pltpu.make_async_copy(view, view, ag_recv).wait()

    @pl.when(me >= pieces)
    def _():
        pltpu.make_async_copy(ag_buf, ag_buf, ag_recv).wait()

    sums_ref[...] = ag_buf[...]

    view = buf.at[pl.ds(0, chips - 1)]
    pltpu.make_async_copy(view, view, send_sem).wait()

    @pl.loop(0, pieces)
    def _(p):
        @pl.when(p != me)
        def _():
            piece_copy(p).wait_send()

    @pl.when(me < pieces)
    def _():
        pltpu.make_async_copy(ag_size, ag_size, ag_send).wait()


def unpack_kernel(fgrad_ref, sums_ref, fgrad_out, gw_in_ref, gb_in_ref, gw_out_ref):
    def unpack(first, count):
        rows = []
        for p in range(first, first + count):
            piece = sums_ref[p].astype(jnp.float32)
            rows.append(jnp.concatenate([piece[:8], piece[8:]], 1))
        return jnp.concatenate(rows, 0) if count > 1 else rows[0]

    in_pieces, out_pieces = gw_in_ref.shape[0] // 8, gw_out_ref.shape[0] // 8
    fgrad_out[...] = fgrad_ref[...]
    gw_in_ref[...] = unpack(0, in_pieces)
    gw_out_ref[...] = unpack(in_pieces, out_pieces)
    gb_in_ref[...] = unpack(in_pieces + out_pieces, 1)[:1]


def solution(mesh):
    R, C = mesh.shape["rows"], mesh.shape["cols"]
    n = R * C

    def body(inputs, task_ids, scale_table, probes, solves, alpha_solve, w_in, b_in, w_out):
        width, trials = inputs.shape
        hidden_width, feat_width = w_out.shape
        pieces = (width + feat_width) // 8 + 1
        operands = (
            inputs, task_ids[None, :], scale_table[None, :], probes, solves, alpha_solve[None, :], w_in, b_in[None, :],
            w_out.T,
        )
        staged = [pltpu.VMEM(a.shape, a.dtype) for a in operands]
        vmem = pl.BlockSpec(memory_space=pltpu.VMEM)
        fgrad, sums = pl.pallas_call(
            functools.partial(whole_kernel, R, C),
            out_shape=(
                jax.ShapeDtypeStruct((feat_width, trials), jnp.float32),
                jax.ShapeDtypeStruct((pieces, 16, LANES), jnp.bfloat16),
            ),
            in_specs=[pl.BlockSpec(memory_space=pltpu.HBM)] * 9,
            out_specs=(vmem,) * 2,
            scratch_shapes=staged
            + [
                pltpu.SemaphoreType.DMA((9,)),
                pltpu.VMEM((n // 2, trials // 2 + 16, LANES), jnp.bfloat16),
                pltpu.VMEM((2, 2, trials, LANES), jnp.bfloat16),
                pltpu.VMEM((2, trials, LANES), jnp.float32),
                pltpu.VMEM((pieces, 16, LANES), jnp.float32),
                pltpu.VMEM((n, 16, LANES), jnp.float32),
                pltpu.VMEM((pieces, 16, LANES), jnp.bfloat16),
                pltpu.VMEM((n - 1, 16, LANES), jnp.bfloat16),
                pltpu.SemaphoreType.DMA((n // 2,)),
                pltpu.SemaphoreType.DMA,
                pltpu.SemaphoreType.DMA((2,)),
                pltpu.SemaphoreType.DMA((2,)),
                pltpu.SemaphoreType.DMA((pieces,)),
                pltpu.SemaphoreType.DMA,
                pltpu.SemaphoreType.DMA,
                pltpu.SemaphoreType.DMA,
            ],
            compiler_params=pltpu.CompilerParams(
                collective_id=0, has_side_effects=True, vmem_limit_bytes=64 * 1024 * 1024
            ),
        )(*operands)
        fgrad, gw_in, gb_in, gw_out = pl.pallas_call(
            unpack_kernel,
            out_shape=(
                jax.ShapeDtypeStruct((feat_width, trials), jnp.float32),
                jax.ShapeDtypeStruct((width, hidden_width), jnp.float32),
                jax.ShapeDtypeStruct((1, hidden_width), jnp.float32),
                jax.ShapeDtypeStruct((feat_width, hidden_width), jnp.float32),
            ),
            in_specs=[vmem] * 2,
            out_specs=(vmem,) * 4,
            compiler_params=pltpu.CompilerParams(vmem_limit_bytes=64 * 1024 * 1024),
        )(fgrad, sums)
        return fgrad, gw_in, gb_in[0], jnp.transpose(gw_out)

    split = ("groups", "rows", "cols")
    return jax.shard_map(
        body,
        mesh=mesh,
        in_specs=(
            P(None, split), P(split), P(), P(None, split), P(None, split), P(split), P(), P(), P(),
        ),
        out_specs=(P(None, split), P("groups", None), P("groups"), P("groups", None)),
        check_vma=False,
    )
```

```python
import functools
import math

import jax
import jax.numpy as jnp
from jax import lax
from jax.experimental import pallas as pl
from jax.experimental.pallas import tpu as pltpu
from jax.sharding import PartitionSpec as P

kernel_rate = 1.0
MESH = pl.DeviceIdType.MESH
LANES = 128


def split3(value):
    high = value.astype(jnp.bfloat16).astype(jnp.float32)
    rest = value - high
    mid = rest.astype(jnp.bfloat16).astype(jnp.float32)
    low = (rest - mid).astype(jnp.bfloat16).astype(jnp.float32)
    return high, mid, low


def whole_kernel(
    R, C,
    *refs_and_scratch,
):
    operands, refs = refs_and_scratch[:9], refs_and_scratch[9:]
    fgrad_ref, sums_ref, *refs = refs
    staged, (load_sem, *refs) = refs[:9], refs[9:]
    inputs_ref, ids_ref, table_ref, probes_ref, solves_ref, alpha_ref, w_in_ref, b_in_ref, w_out_t_ref = staged
    (
        buf, left_buf, swap, parts, rs_buf, ag_buf, ag_size,
        recv_sem, send_sem, core_send, core_recv, rs_send, rs_recv, ag_send, ag_recv,
    ) = refs
    n = R * C
    r, c = lax.axis_index("rows"), lax.axis_index("cols")
    me = r * C + c
    trials = inputs_ref.shape[1]
    feat_width = w_out_t_ref.shape[0]
    probe_count = probes_ref.shape[0]
    pieces = parts.shape[0]

    def coords(q):
        return {"rows": q // C, "cols": lax.rem(q, C)}

    def other(k):
        return lax.rem(me + k, n)

    barrier = pltpu.get_barrier_semaphore()

    @pl.loop(1, n)
    def _(k):
        pl.semaphore_signal(barrier, inc=1, device_id=coords(other(k)), device_id_type=MESH)

    loads = [
        pltpu.make_async_copy(operands[k], staged[k], load_sem.at[k]) for k in range(9)
    ]
    for load in loads:
        load.start()

    for load in loads:
        load.wait()

    ids = ids_ref[...]
    lo, hi = lax.rem(ids, LANES), ids // LANES
    flat = table_ref[...]
    tasks = flat.shape[1]
    groups = -(-tasks // (8 * LANES)) * 8
    flat = jnp.concatenate([flat, jnp.zeros((1, groups * LANES - tasks), jnp.float32)], 1)
    table = jnp.concatenate([flat[:, k * LANES : (k + 1) * LANES] for k in range(groups)], 0)
    hot = (lax.broadcasted_iota(jnp.int32, (LANES, trials), 0) == lo).astype(jnp.float32).astype(jnp.bfloat16)
    terms = jnp.concatenate(split3(table), 0).astype(jnp.bfloat16)
    found = jnp.dot(terms, hot, preferred_element_type=jnp.float32)
    found = found[:groups] + found[groups : 2 * groups] + found[2 * groups :]
    mine = lax.broadcasted_iota(jnp.int32, (groups, trials), 0) == hi
    scale = jnp.sum(jnp.where(mine, found, 0.0), 0, keepdims=True)

    inputs = inputs_ref[...]
    width, half = inputs.shape[0], trials // 2
    raw_lanes = width + 2 * probe_count
    pad = -trials % LANES
    raw = jnp.concatenate(
        [
            inputs.astype(jnp.float32),
            solves_ref[...] * scale,
            probes_ref[...] * scale,
            jnp.broadcast_to(alpha_ref[...] * scale, (LANES - raw_lanes, trials)),
        ],
        0,
    )
    raw = jnp.transpose(jnp.concatenate([raw, jnp.zeros((LANES, pad), jnp.float32)], 1))[:trials]
    raw = raw.astype(jnp.bfloat16).astype(jnp.float32)

    chips = n // 2
    here, side = r * (C // 2) + c // 2, lax.rem(c, 2)
    main_part = jnp.concatenate([raw[:half, :raw_lanes], raw[half:, :raw_lanes]], 1)
    tile_lane = lax.broadcasted_iota(jnp.int32, (16, LANES), 1)
    a_part = jnp.zeros((16, LANES), jnp.float32)
    for k in range(trials // 16):
        a_part = jnp.where(tile_lane == k, raw[16 * k : 16 * k + 16, raw_lanes : raw_lanes + 1], a_part)
    buf[here, :half] = main_part.astype(jnp.bfloat16)
    buf[here, half:] = a_part.astype(jnp.bfloat16)

    pl.semaphore_wait(barrier, n - 1)

    def send(k):
        chip = here ^ k
        pltpu.make_async_remote_copy(
            src_ref=buf.at[here], dst_ref=buf.at[here], send_sem=send_sem, recv_sem=recv_sem.at[here],
            device_id={"rows": chip // (C // 2), "cols": lax.rem(chip, C // 2) * 2 + side},
            device_id_type=MESH,
        ).start()

    far = chips // 2

    @pl.loop(far, chips)
    def _(k):
        send(k)

    @pl.loop(1, far)
    def _(k):
        send(k)

    w_in, b_in = w_in_ref[...], b_in_ref[...]
    hidden_width = w_in.shape[1]
    preact = lax.dot_general(
        inputs, w_in, (((0,), (0,)), ((), ())), preferred_element_type=jnp.float32
    ) + b_in
    sig = 1.0 / (1.0 + jnp.exp(-preact))
    hidden = (preact * sig).astype(jnp.bfloat16)
    w_out_t = w_out_t_ref[...]
    feats = lax.dot_general(
        hidden, w_out_t, (((1,), (1,)), ((), ())), preferred_element_type=jnp.float32
    ).astype(jnp.bfloat16)
    feats_f = feats.astype(jnp.float32)
    sqnorm = jnp.sum(feats_f * feats_f, 1, keepdims=True)
    vecs = raw[:, width : width + LANES - feat_width]

    first_u, first_z = feat_width, feat_width + probe_count
    at_a = feat_width + 2 * probe_count
    lane = lax.broadcasted_iota(jnp.int32, (trials, LANES), 1)
    n_hi, n_mid, n_lo = split3(sqnorm)
    base = jnp.concatenate([feats_f, vecs], 1)
    rate = kernel_rate / feat_width
    row_exp = jnp.where(
        lane < feat_width,
        base * (2.0 * rate),
        jnp.where(
            lane <= at_a, 0.0,
            jnp.where(
                lane <= at_a + 3, -rate,
                jnp.where(
                    lane == at_a + 4, n_hi * -rate,
                    jnp.where(
                        lane == at_a + 5, n_mid * -rate,
                        jnp.where(lane == at_a + 6, n_lo * -rate, 0.0),
                    ),
                ),
            ),
        ),
    )
    swapped = jnp.concatenate(
        [feats_f, vecs[:, probe_count : 2 * probe_count], vecs[:, :probe_count], vecs[:, 2 * probe_count :]], 1
    )
    row_pair = jnp.where(
        lane < feat_width, 0.0,
        jnp.where(lane < at_a, swapped * (0.5 / probe_count), jnp.where(lane == at_a, -swapped, 0.0)),
    )
    left_buf[0, 0] = row_exp.astype(jnp.bfloat16)
    left_buf[0, 1] = row_pair.astype(jnp.bfloat16)

    def core_copy(refs, which):
        return pltpu.make_async_remote_copy(
            src_ref=refs.at[0], dst_ref=refs.at[1], send_sem=core_send.at[which], recv_sem=core_recv.at[which],
            device_id={"rows": r, "cols": c ^ 1}, device_id_type=MESH,
        )

    def wait_chip(k):
        chip = here ^ k
        pltpu.make_async_copy(buf.at[chip], buf.at[chip], recv_sem.at[chip]).wait()

    core_copy(left_buf, 0).start()
    core_copy(left_buf, 0).wait()
    left = jnp.concatenate([left_buf[0, 0], left_buf[1, 0], left_buf[0, 1], left_buf[1, 1]], 0)

    blank = jnp.zeros((width, hidden_width), jnp.bfloat16)
    gap = jnp.zeros((2 * probe_count, 2 * hidden_width), jnp.bfloat16)
    first_layer = jnp.concatenate(
        [
            jnp.concatenate([w_in, blank], 1),
            gap,
            jnp.concatenate([blank, w_in], 1),
            gap,
        ],
        0,
    )
    bias = jnp.concatenate([b_in, b_in], 1)
    second_layer = jnp.concatenate([w_out_t, jnp.zeros((LANES - feat_width, hidden_width), jnp.bfloat16)], 0)
    s_row = lax.broadcasted_iota(jnp.int32, (2 * LANES, LANES), 0)
    s_lane = lax.broadcasted_iota(jnp.int32, (2 * LANES, LANES), 1)
    lane2 = lax.broadcasted_iota(jnp.int32, (trials, LANES), 1)
    block = lax.rem(lax.broadcasted_iota(jnp.int32, (trials, LANES), 0), half) // 16
    places, a_masks = [], []
    for h in range(2):
        vec_place = (s_row == s_lane - feat_width + width + h * raw_lanes) & (s_lane >= feat_width) & (s_lane < at_a)
        place = vec_place | ((s_row >= LANES) & (s_lane == at_a))
        places.append(place.astype(jnp.float32).astype(jnp.bfloat16))
        a_masks.append((lane2 == block + h * (half // 16)).astype(jnp.float32).astype(jnp.bfloat16))

    def columns(pair):
        blocks = buf[pl.ds(2 * pair, 2)]
        main = blocks[:, :half].reshape(trials, LANES)
        tiles = jnp.concatenate([blocks[0, half:]] * (half // 16) + [blocks[1, half:]] * (half // 16), 0)
        pre = jnp.dot(main, first_layer, preferred_element_type=jnp.float32) + bias
        hid = (pre * (1.0 / (1.0 + jnp.exp(-pre)))).astype(jnp.bfloat16)
        found = []
        for h in range(2):
            value = lax.dot_general(
                hid[:, h * hidden_width : (h + 1) * hidden_width], second_layer,
                (((1,), (1,)), ((), ())), preferred_element_type=jnp.float32,
            ) + jnp.dot(
                jnp.concatenate([main, tiles * a_masks[h]], 1), places[h], preferred_element_type=jnp.float32
            )
            value = value.astype(jnp.bfloat16).astype(jnp.float32)
            norm = jnp.sum(jnp.where(lane2 < feat_width, value * value, 0.0), 1, keepdims=True)
            high, mid, low = split3(norm)
            found.append(
                jnp.where(
                    lane2 <= at_a, value,
                    jnp.where(
                        lane2 == at_a + 1, high,
                        jnp.where(
                            lane2 == at_a + 2, mid,
                            jnp.where(lane2 == at_a + 3, low, jnp.where(lane2 <= at_a + 6, 1.0, 0.0)),
                        ),
                    ),
                )
            )
        return jnp.concatenate(found, 0).astype(jnp.bfloat16)

    def add_pair(p, carry):
        total, sums = carry
        cols = columns((here // 2) ^ p)
        both = lax.dot_general(left, cols, (((1,), (1,)), ((), ())), preferred_element_type=jnp.float32)
        weight = both[2 * trials :] * jnp.exp(both[: 2 * trials])
        for j in range(2 * trials // LANES):
            sums = sums + weight[:, j * LANES : (j + 1) * LANES]
        total = total + jnp.dot(weight.astype(jnp.bfloat16), cols, preferred_element_type=jnp.float32)
        return total, sums

    def step(p, carry):
        wait_chip(2 * p)
        wait_chip(2 * p + 1)
        return add_pair(p, carry)

    empty = jnp.zeros((2 * trials, LANES), jnp.float32)
    wait_chip(1)
    carry = add_pair(0, (empty, empty))
    total, sums = lax.fori_loop(1, chips // 2, step, carry)

    weight_sum = jnp.sum(sums, 1, keepdims=True)
    lane4 = lax.broadcasted_iota(jnp.int32, (2 * trials, LANES), 1)
    mixed = jnp.where(lane4 < feat_width, total, weight_sum)
    swap[0] = mixed[trials:]
    core_copy(swap, 1).start()
    core_copy(swap, 1).wait()
    mixed = mixed[:trials] + swap[1]
    total, weight_sum = mixed[:, :feat_width], mixed[:, feat_width : feat_width + 1]
    feat_grad = (total - weight_sum * feats_f) * (2.0 * rate)
    grad_feats = feat_grad.astype(jnp.bfloat16)
    order = sorted(range(R), key=lambda k: abs(2 * k - R + 1))[:2]
    owners = len(order) * C
    rank = jnp.where(r == order[0], c, jnp.where(r == order[-1], (len(order) - 1) * C + c, owners))
    held = -(-pieces // owners)

    def owner(p):
        q = lax.rem(p, owners)
        return {"rows": jnp.where(q < C, order[0], order[-1]), "cols": lax.rem(q, C)}

    def piece_copy(p):
        return pltpu.make_async_remote_copy(
            src_ref=parts.at[p], dst_ref=rs_buf.at[p // owners, me], send_sem=rs_send.at[p],
            recv_sem=rs_recv.at[p // owners], device_id=owner(p), device_id_type=MESH,
        )

    def send_pieces(values, first):
        count = values.shape[0] // 8
        for p in range(count):
            for h in range(2):
                part = values[8 * p : 8 * p + 8, h * LANES : (h + 1) * LANES]
                parts[first + p, 8 * h : 8 * h + 8] = part.astype(parts.dtype)

        @pl.loop(first, first + count)
        def _(p):
            @pl.when(lax.rem(p, owners) != rank)
            def _():
                piece_copy(p).start()

    g_out = lax.dot_general(
        grad_feats, hidden, (((0,), (0,)), ((), ())), preferred_element_type=jnp.float32
    )
    send_pieces(g_out, 0)
    grad_hidden = jnp.dot(grad_feats, w_out_t, preferred_element_type=jnp.float32)
    grad_pre = grad_hidden * (sig * (1.0 + preact * (1.0 - sig)))
    g_in = jnp.dot(inputs, grad_pre.astype(jnp.bfloat16), preferred_element_type=jnp.float32)
    g_bias = jnp.broadcast_to(jnp.sum(grad_pre, 0, keepdims=True), (8, grad_pre.shape[1]))
    send_pieces(jnp.concatenate([g_in, g_bias], 0), feat_width // 8)

    wide = jnp.concatenate([feat_grad, jnp.zeros((trials, LANES - feat_width), jnp.float32)], 1)
    wide = jnp.concatenate([wide, jnp.zeros((pad, LANES), jnp.float32)], 0)
    fgrad_ref[...] = jnp.transpose(wide)[:feat_width, :trials]

    def ag_copy(p, k):
        return pltpu.make_async_remote_copy(
            src_ref=ag_buf.at[p], dst_ref=ag_buf.at[p], send_sem=ag_send.at[p // owners], recv_sem=ag_recv.at[p],
            device_id=coords(other(k)), device_id_type=MESH,
        )

    factor = 1.0 / math.sqrt(trials * n)
    for h in range(held):
        p = rank + h * owners

        @pl.when((rank < owners) & (p < pieces))
        def _():
            rs_buf[h, me] = parts[p]
            view = rs_buf.at[h, pl.ds(0, n - 1)]
            pltpu.make_async_copy(view, view, rs_recv.at[h]).wait()
            summed = jnp.sum(rs_buf[h].astype(jnp.float32), 0) * factor
            ag_buf[p] = summed.astype(jnp.bfloat16)

            @pl.loop(1, n)
            def _(k):
                ag_copy(p, k).start()

    @pl.loop(0, pieces)
    def _(p):
        @pl.when(lax.rem(p, owners) != rank)
        def _():
            pltpu.make_async_copy(ag_buf.at[p], ag_buf.at[p], ag_recv.at[p]).wait()

    sums_ref[...] = ag_buf[...]

    view = buf.at[pl.ds(0, chips - 1)]
    pltpu.make_async_copy(view, view, send_sem).wait()

    @pl.loop(0, pieces)
    def _(p):
        @pl.when(lax.rem(p, owners) != rank)
        def _():
            piece_copy(p).wait_send()

    for h in range(held):
        @pl.when((rank < owners) & (rank + h * owners < pieces))
        def _():
            pltpu.make_async_copy(ag_size, ag_size, ag_send.at[h]).wait()


def unpack_kernel(fgrad_ref, sums_ref, fgrad_out, gw_in_ref, gb_in_ref, gw_out_ref):
    def unpack(first, count):
        rows = []
        for p in range(first, first + count):
            piece = sums_ref[p].astype(jnp.float32)
            rows.append(jnp.concatenate([piece[:8], piece[8:]], 1))
        return jnp.concatenate(rows, 0) if count > 1 else rows[0]

    in_pieces, out_pieces = gw_in_ref.shape[0] // 8, gw_out_ref.shape[0] // 8
    fgrad_out[...] = fgrad_ref[...]
    gw_out_ref[...] = unpack(0, out_pieces)
    gw_in_ref[...] = unpack(out_pieces, in_pieces)
    gb_in_ref[...] = unpack(in_pieces + out_pieces, 1)[:1]


def solution(mesh):
    R, C = mesh.shape["rows"], mesh.shape["cols"]
    n = R * C

    def body(inputs, task_ids, scale_table, probes, solves, alpha_solve, w_in, b_in, w_out):
        width, trials = inputs.shape
        hidden_width, feat_width = w_out.shape
        pieces = (width + feat_width) // 8 + 1
        operands = (
            inputs, task_ids[None, :], scale_table[None, :], probes, solves, alpha_solve[None, :], w_in, b_in[None, :],
            w_out.T,
        )
        staged = [pltpu.VMEM(a.shape, a.dtype) for a in operands]
        held = -(-pieces // (min(R, 2) * C))
        vmem = pl.BlockSpec(memory_space=pltpu.VMEM)
        fgrad, sums = pl.pallas_call(
            functools.partial(whole_kernel, R, C),
            out_shape=(
                jax.ShapeDtypeStruct((feat_width, trials), jnp.float32),
                jax.ShapeDtypeStruct((pieces, 16, LANES), jnp.bfloat16),
            ),
            in_specs=[pl.BlockSpec(memory_space=pltpu.HBM)] * 9,
            out_specs=(vmem,) * 2,
            scratch_shapes=staged
            + [
                pltpu.SemaphoreType.DMA((9,)),
                pltpu.VMEM((n // 2, trials // 2 + 16, LANES), jnp.bfloat16),
                pltpu.VMEM((2, 2, trials, LANES), jnp.bfloat16),
                pltpu.VMEM((2, trials, LANES), jnp.float32),
                pltpu.VMEM((pieces, 16, LANES), jnp.bfloat16),
                pltpu.VMEM((held, n, 16, LANES), jnp.bfloat16),
                pltpu.VMEM((pieces, 16, LANES), jnp.bfloat16),
                pltpu.VMEM((n - 1, 16, LANES), jnp.bfloat16),
                pltpu.SemaphoreType.DMA((n // 2,)),
                pltpu.SemaphoreType.DMA,
                pltpu.SemaphoreType.DMA((2,)),
                pltpu.SemaphoreType.DMA((2,)),
                pltpu.SemaphoreType.DMA((pieces,)),
                pltpu.SemaphoreType.DMA((held,)),
                pltpu.SemaphoreType.DMA((held,)),
                pltpu.SemaphoreType.DMA((pieces,)),
            ],
            compiler_params=pltpu.CompilerParams(
                collective_id=0, has_side_effects=True, vmem_limit_bytes=48 * 1024 * 1024
            ),
        )(*[pltpu.with_memory_space_constraint(a, pltpu.HBM) for a in operands])
        fgrad, gw_in, gb_in, gw_out = pl.pallas_call(
            unpack_kernel,
            out_shape=(
                jax.ShapeDtypeStruct((feat_width, trials), jnp.float32),
                jax.ShapeDtypeStruct((width, hidden_width), jnp.float32),
                jax.ShapeDtypeStruct((1, hidden_width), jnp.float32),
                jax.ShapeDtypeStruct((feat_width, hidden_width), jnp.float32),
            ),
            in_specs=[vmem] * 2,
            out_specs=(vmem,) * 4,
            compiler_params=pltpu.CompilerParams(vmem_limit_bytes=4 * 1024 * 1024),
        )(fgrad, sums)
        return fgrad, gw_in, gb_in[0], jnp.transpose(gw_out)

    split = ("groups", "rows", "cols")
    return jax.shard_map(
        body,
        mesh=mesh,
        in_specs=(
            P(None, split), P(split), P(), P(None, split), P(None, split), P(split), P(), P(), P(),
        ),
        out_specs=(P(None, split), P("groups", None), P("groups"), P("groups", None)),
        check_vma=False,
    )
```

```python
import functools
import math

import jax
import jax.numpy as jnp
from jax import lax
from jax.experimental import pallas as pl
from jax.experimental.pallas import tpu as pltpu
from jax.sharding import PartitionSpec as P

kernel_rate = 1.0
MESH = pl.DeviceIdType.MESH
LANES = 128


def split3(value):
    high = value.astype(jnp.bfloat16).astype(jnp.float32)
    rest = value - high
    mid = rest.astype(jnp.bfloat16).astype(jnp.float32)
    low = (rest - mid).astype(jnp.bfloat16).astype(jnp.float32)
    return high, mid, low


def whole_kernel(
    R, C,
    *refs_and_scratch,
):
    operands, refs = refs_and_scratch[:9], refs_and_scratch[9:]
    fgrad_ref, sums_ref, *refs = refs
    staged, (load_sem, *refs) = refs[:9], refs[9:]
    inputs_ref, ids_ref, table_ref, probes_ref, solves_ref, alpha_ref, w_in_ref, b_in_ref, w_out_t_ref = staged
    (
        buf, left_buf, swap, parts, rs_buf, ag_buf, ag_size,
        recv_sem, send_sem, core_send, core_recv, rs_send, rs_recv, ag_send, ag_recv,
    ) = refs
    n = R * C
    r, c = lax.axis_index("rows"), lax.axis_index("cols")
    me = r * C + c
    trials = inputs_ref.shape[1]
    feat_width = w_out_t_ref.shape[0]
    probe_count = probes_ref.shape[0]
    pieces = parts.shape[0]

    def coords(q):
        return {"rows": q // C, "cols": lax.rem(q, C)}

    def other(k):
        return lax.rem(me + k, n)

    barrier = pltpu.get_barrier_semaphore()

    @pl.loop(1, n)
    def _(k):
        pl.semaphore_signal(barrier, inc=1, device_id=coords(other(k)), device_id_type=MESH)

    loads = [
        pltpu.make_async_copy(operands[k], staged[k], load_sem.at[k]) for k in range(9)
    ]
    for load in loads:
        load.start()

    for load in loads:
        load.wait()

    ids = ids_ref[...]
    lo, hi = lax.rem(ids, LANES), ids // LANES
    flat = table_ref[...]
    tasks = flat.shape[1]
    groups = -(-tasks // (8 * LANES)) * 8
    flat = jnp.concatenate([flat, jnp.zeros((1, groups * LANES - tasks), jnp.float32)], 1)
    table = jnp.concatenate([flat[:, k * LANES : (k + 1) * LANES] for k in range(groups)], 0)
    hot = (lax.broadcasted_iota(jnp.int32, (LANES, trials), 0) == lo).astype(jnp.float32).astype(jnp.bfloat16)
    terms = jnp.concatenate(split3(table), 0).astype(jnp.bfloat16)
    found = jnp.dot(terms, hot, preferred_element_type=jnp.float32)
    found = found[:groups] + found[groups : 2 * groups] + found[2 * groups :]
    mine = lax.broadcasted_iota(jnp.int32, (groups, trials), 0) == hi
    scale = jnp.sum(jnp.where(mine, found, 0.0), 0, keepdims=True)

    inputs = inputs_ref[...]
    width, half = inputs.shape[0], trials // 2
    raw_lanes = width + 2 * probe_count
    pad = -trials % LANES
    raw = jnp.concatenate(
        [
            inputs.astype(jnp.float32),
            solves_ref[...] * scale,
            probes_ref[...] * scale,
            jnp.broadcast_to(alpha_ref[...] * scale, (LANES - raw_lanes, trials)),
        ],
        0,
    )
    raw = jnp.transpose(jnp.concatenate([raw, jnp.zeros((LANES, pad), jnp.float32)], 1))[:trials]
    raw = raw.astype(jnp.bfloat16).astype(jnp.float32)

    chips = n // 2
    here, side = r * (C // 2) + c // 2, lax.rem(c, 2)
    main_part = jnp.concatenate([raw[:half, :raw_lanes], raw[half:, :raw_lanes]], 1)
    tile_lane = lax.broadcasted_iota(jnp.int32, (16, LANES), 1)
    a_part = jnp.zeros((16, LANES), jnp.float32)
    for k in range(trials // 16):
        a_part = jnp.where(tile_lane == k, raw[16 * k : 16 * k + 16, raw_lanes : raw_lanes + 1], a_part)
    buf[here, :half] = main_part.astype(jnp.bfloat16)
    buf[here, half:] = a_part.astype(jnp.bfloat16)

    pl.semaphore_wait(barrier, n - 1)

    def send(k):
        chip = here ^ k
        pltpu.make_async_remote_copy(
            src_ref=buf.at[here], dst_ref=buf.at[here], send_sem=send_sem, recv_sem=recv_sem.at[here],
            device_id={"rows": chip // (C // 2), "cols": lax.rem(chip, C // 2) * 2 + side},
            device_id_type=MESH,
        ).start()

    far = chips // 2

    @pl.loop(far, chips)
    def _(k):
        send(k)

    @pl.loop(1, far)
    def _(k):
        send(k)

    w_in, b_in = w_in_ref[...], b_in_ref[...]
    hidden_width = w_in.shape[1]
    preact = lax.dot_general(
        inputs, w_in, (((0,), (0,)), ((), ())), preferred_element_type=jnp.float32
    ) + b_in
    sig = 1.0 / (1.0 + jnp.exp(-preact))
    hidden = (preact * sig).astype(jnp.bfloat16)
    w_out_t = w_out_t_ref[...]
    feats = lax.dot_general(
        hidden, w_out_t, (((1,), (1,)), ((), ())), preferred_element_type=jnp.float32
    ).astype(jnp.bfloat16)
    feats_f = feats.astype(jnp.float32)
    sqnorm = jnp.sum(feats_f * feats_f, 1, keepdims=True)
    vecs = raw[:, width : width + LANES - feat_width]

    first_u, first_z = feat_width, feat_width + probe_count
    at_a = feat_width + 2 * probe_count
    lane = lax.broadcasted_iota(jnp.int32, (trials, LANES), 1)
    n_hi, n_mid, n_lo = split3(sqnorm)
    base = jnp.concatenate([feats_f, vecs], 1)
    rate = kernel_rate / feat_width
    row_exp = jnp.where(
        lane < feat_width,
        base * (2.0 * rate),
        jnp.where(
            lane <= at_a, 0.0,
            jnp.where(
                lane <= at_a + 3, -rate,
                jnp.where(
                    lane == at_a + 4, n_hi * -rate,
                    jnp.where(
                        lane == at_a + 5, n_mid * -rate,
                        jnp.where(lane == at_a + 6, n_lo * -rate, 0.0),
                    ),
                ),
            ),
        ),
    )
    swapped = jnp.concatenate(
        [feats_f, vecs[:, probe_count : 2 * probe_count], vecs[:, :probe_count], vecs[:, 2 * probe_count :]], 1
    )
    row_pair = jnp.where(
        lane < feat_width, 0.0,
        jnp.where(lane < at_a, swapped * (0.5 / probe_count), jnp.where(lane == at_a, -swapped, 0.0)),
    )
    left_buf[0, 0] = row_exp.astype(jnp.bfloat16)
    left_buf[0, 1] = row_pair.astype(jnp.bfloat16)

    def core_copy(refs, which):
        return pltpu.make_async_remote_copy(
            src_ref=refs.at[0], dst_ref=refs.at[1], send_sem=core_send.at[which], recv_sem=core_recv.at[which],
            device_id={"rows": r, "cols": c ^ 1}, device_id_type=MESH,
        )

    def wait_chip(k):
        chip = here ^ k
        pltpu.make_async_copy(buf.at[chip], buf.at[chip], recv_sem.at[chip]).wait()

    core_copy(left_buf, 0).start()
    core_copy(left_buf, 0).wait()
    left = jnp.concatenate([left_buf[0, 0], left_buf[1, 0], left_buf[0, 1], left_buf[1, 1]], 0)

    blank = jnp.zeros((width, hidden_width), jnp.bfloat16)
    gap = jnp.zeros((2 * probe_count, 2 * hidden_width), jnp.bfloat16)
    first_layer = jnp.concatenate(
        [
            jnp.concatenate([w_in, blank], 1),
            gap,
            jnp.concatenate([blank, w_in], 1),
            gap,
        ],
        0,
    )
    bias = jnp.concatenate([b_in, b_in], 1)
    second_layer = jnp.concatenate([w_out_t, jnp.zeros((LANES - feat_width, hidden_width), jnp.bfloat16)], 0)
    s_row = lax.broadcasted_iota(jnp.int32, (2 * LANES, LANES), 0)
    s_lane = lax.broadcasted_iota(jnp.int32, (2 * LANES, LANES), 1)
    lane2 = lax.broadcasted_iota(jnp.int32, (trials, LANES), 1)
    block = lax.rem(lax.broadcasted_iota(jnp.int32, (trials, LANES), 0), half) // 16
    places, a_masks = [], []
    for h in range(2):
        vec_place = (s_row == s_lane - feat_width + width + h * raw_lanes) & (s_lane >= feat_width) & (s_lane < at_a)
        place = vec_place | ((s_row >= LANES) & (s_lane == at_a))
        places.append(place.astype(jnp.float32).astype(jnp.bfloat16))
        a_masks.append((lane2 == block + h * (half // 16)).astype(jnp.float32).astype(jnp.bfloat16))

    def columns(pair):
        blocks = buf[pl.ds(2 * pair, 2)]
        main = blocks[:, :half].reshape(trials, LANES)
        tiles = jnp.concatenate([blocks[0, half:]] * (half // 16) + [blocks[1, half:]] * (half // 16), 0)
        pre = jnp.dot(main, first_layer, preferred_element_type=jnp.float32) + bias
        hid = (pre * (1.0 / (1.0 + jnp.exp(-pre)))).astype(jnp.bfloat16)
        found = []
        for h in range(2):
            value = lax.dot_general(
                hid[:, h * hidden_width : (h + 1) * hidden_width], second_layer,
                (((1,), (1,)), ((), ())), preferred_element_type=jnp.float32,
            ) + jnp.dot(
                jnp.concatenate([main, tiles * a_masks[h]], 1), places[h], preferred_element_type=jnp.float32
            )
            value = value.astype(jnp.bfloat16).astype(jnp.float32)
            norm = jnp.sum(jnp.where(lane2 < feat_width, value * value, 0.0), 1, keepdims=True)
            high, mid, low = split3(norm)
            found.append(
                jnp.where(
                    lane2 <= at_a, value,
                    jnp.where(
                        lane2 == at_a + 1, high,
                        jnp.where(
                            lane2 == at_a + 2, mid,
                            jnp.where(lane2 == at_a + 3, low, jnp.where(lane2 <= at_a + 6, 1.0, 0.0)),
                        ),
                    ),
                )
            )
        return jnp.concatenate(found, 0).astype(jnp.bfloat16)

    def add_columns(cols, total, sums):
        both = lax.dot_general(left, cols, (((1,), (1,)), ((), ())), preferred_element_type=jnp.float32)
        weight = both[2 * trials :] * jnp.exp(both[: 2 * trials])
        for j in range(2 * trials // LANES):
            sums = sums + weight[:, j * LANES : (j + 1) * LANES]
        total = total + jnp.dot(weight.astype(jnp.bfloat16), cols, preferred_element_type=jnp.float32)
        return total, sums

    def step(p, carry):
        cols, total, sums = carry
        wait_chip(2 * p)
        wait_chip(2 * p + 1)
        later = columns((here // 2) ^ p)
        return (later, *add_columns(cols, total, sums))

    empty = jnp.zeros((2 * trials, LANES), jnp.float32)
    wait_chip(1)
    carry = (columns(here // 2), empty, empty)
    for p in range(1, chips // 2):
        carry = step(p, carry)
    total, sums = add_columns(*carry)

    def share(first):
        weight_sum = jnp.sum(sums[first : first + trials], 1, keepdims=True)
        return jnp.where(lane2 < feat_width, total[first : first + trials], weight_sum)

    swap[0] = share(trials)
    core_copy(swap, 1).start()
    mixed = share(0)
    core_copy(swap, 1).wait()
    mixed = mixed + swap[1]
    total, weight_sum = mixed[:, :feat_width], mixed[:, feat_width : feat_width + 1]
    feat_grad = (total - weight_sum * feats_f) * (2.0 * rate)
    grad_feats = feat_grad.astype(jnp.bfloat16)
    order = sorted(range(R), key=lambda k: abs(2 * k - R + 1))[:2]
    owners = len(order) * C
    rank = jnp.where(r == order[0], c, jnp.where(r == order[-1], (len(order) - 1) * C + c, owners))
    held = -(-pieces // owners)

    def owner(p):
        q = lax.rem(p, owners)
        return {"rows": jnp.where(q < C, order[0], order[-1]), "cols": lax.rem(q, C)}

    def piece_copy(p):
        return pltpu.make_async_remote_copy(
            src_ref=parts.at[p], dst_ref=rs_buf.at[p // owners, me], send_sem=rs_send.at[p],
            recv_sem=rs_recv.at[p // owners], device_id=owner(p), device_id_type=MESH,
        )

    def send_pieces(values, first):
        count = values.shape[0] // 8
        for p in range(count):
            for h in range(2):
                part = values[8 * p : 8 * p + 8, h * LANES : (h + 1) * LANES]
                parts[first + p, 8 * h : 8 * h + 8] = part.astype(parts.dtype)

        @pl.loop(first, first + count)
        def _(p):
            @pl.when(lax.rem(p, owners) != rank)
            def _():
                piece_copy(p).start()

    g_out = lax.dot_general(
        grad_feats, hidden, (((0,), (0,)), ((), ())), preferred_element_type=jnp.float32
    )
    send_pieces(g_out, 0)
    grad_hidden = jnp.dot(grad_feats, w_out_t, preferred_element_type=jnp.float32)
    grad_pre = grad_hidden * (sig * (1.0 + preact * (1.0 - sig)))
    g_in = jnp.dot(inputs, grad_pre.astype(jnp.bfloat16), preferred_element_type=jnp.float32)
    bias_terms = split3(jnp.sum(grad_pre, 0, keepdims=True))
    g_bias = jnp.concatenate([*bias_terms, jnp.zeros((5, hidden_width), jnp.float32)], 0)
    send_pieces(jnp.concatenate([g_in, g_bias], 0), feat_width // 8)

    wide = jnp.concatenate([feat_grad, jnp.zeros((trials, LANES - feat_width), jnp.float32)], 1)
    wide = jnp.concatenate([wide, jnp.zeros((pad, LANES), jnp.float32)], 0)
    fgrad_ref[...] = jnp.transpose(wide)[:feat_width, :trials]

    def ag_copy(p, k):
        return pltpu.make_async_remote_copy(
            src_ref=ag_buf.at[p], dst_ref=ag_buf.at[p], send_sem=ag_send.at[p // owners], recv_sem=ag_recv.at[p],
            device_id=coords(other(k)), device_id_type=MESH,
        )

    factor = 1.0 / math.sqrt(trials * n)
    for h in range(held):
        p = rank + h * owners

        @pl.when((rank < owners) & (p < pieces))
        def _():
            rs_buf[h, me] = parts[p]
            view = rs_buf.at[h, pl.ds(0, n - 1)]
            pltpu.make_async_copy(view, view, rs_recv.at[h]).wait()
            summed = jnp.sum(rs_buf[h].astype(jnp.float32), 0) * factor
            ag_buf[p] = summed.astype(jnp.bfloat16)

            @pl.loop(1, n)
            def _(k):
                ag_copy(p, k).start()

    @pl.loop(0, pieces)
    def _(p):
        @pl.when(lax.rem(p, owners) != rank)
        def _():
            pltpu.make_async_copy(ag_buf.at[p], ag_buf.at[p], ag_recv.at[p]).wait()

    sums_ref[...] = ag_buf[...]

    view = buf.at[pl.ds(0, chips - 1)]
    pltpu.make_async_copy(view, view, send_sem).wait()

    @pl.loop(0, pieces)
    def _(p):
        @pl.when(lax.rem(p, owners) != rank)
        def _():
            piece_copy(p).wait_send()

    for h in range(held):
        @pl.when((rank < owners) & (rank + h * owners < pieces))
        def _():
            pltpu.make_async_copy(ag_size, ag_size, ag_send.at[h]).wait()


def unpack_kernel(fgrad_ref, sums_ref, fgrad_out, gw_in_ref, gb_in_ref, gw_out_ref):
    def unpack(first, count):
        rows = []
        for p in range(first, first + count):
            piece = sums_ref[p].astype(jnp.float32)
            rows.append(jnp.concatenate([piece[:8], piece[8:]], 1))
        return jnp.concatenate(rows, 0) if count > 1 else rows[0]

    in_pieces, out_pieces = gw_in_ref.shape[0] // 8, gw_out_ref.shape[0] // 8
    fgrad_out[...] = fgrad_ref[...]
    gw_out_ref[...] = unpack(0, out_pieces)
    gw_in_ref[...] = unpack(out_pieces, in_pieces)
    gb_in_ref[...] = jnp.sum(unpack(in_pieces + out_pieces, 1), 0, keepdims=True)


def solution(mesh):
    R, C = mesh.shape["rows"], mesh.shape["cols"]
    n = R * C

    def body(inputs, task_ids, scale_table, probes, solves, alpha_solve, w_in, b_in, w_out):
        width, trials = inputs.shape
        hidden_width, feat_width = w_out.shape
        pieces = (width + feat_width) // 8 + 1
        operands = (
            inputs, task_ids[None, :], scale_table[None, :], probes, solves, alpha_solve[None, :], w_in, b_in[None, :],
            w_out.T,
        )
        staged = [pltpu.VMEM(a.shape, a.dtype) for a in operands]
        held = -(-pieces // (min(R, 2) * C))
        vmem = pl.BlockSpec(memory_space=pltpu.VMEM)
        fgrad, sums = pl.pallas_call(
            functools.partial(whole_kernel, R, C),
            out_shape=(
                jax.ShapeDtypeStruct((feat_width, trials), jnp.float32),
                jax.ShapeDtypeStruct((pieces, 16, LANES), jnp.bfloat16),
            ),
            in_specs=[pl.BlockSpec(memory_space=pltpu.HBM)] * 9,
            out_specs=(vmem,) * 2,
            scratch_shapes=staged
            + [
                pltpu.SemaphoreType.DMA((9,)),
                pltpu.VMEM((n // 2, trials // 2 + 16, LANES), jnp.bfloat16),
                pltpu.VMEM((2, 2, trials, LANES), jnp.bfloat16),
                pltpu.VMEM((2, trials, LANES), jnp.float32),
                pltpu.VMEM((pieces, 16, LANES), jnp.bfloat16),
                pltpu.VMEM((held, n, 16, LANES), jnp.bfloat16),
                pltpu.VMEM((pieces, 16, LANES), jnp.bfloat16),
                pltpu.VMEM((n - 1, 16, LANES), jnp.bfloat16),
                pltpu.SemaphoreType.DMA((n // 2,)),
                pltpu.SemaphoreType.DMA,
                pltpu.SemaphoreType.DMA((2,)),
                pltpu.SemaphoreType.DMA((2,)),
                pltpu.SemaphoreType.DMA((pieces,)),
                pltpu.SemaphoreType.DMA((held,)),
                pltpu.SemaphoreType.DMA((held,)),
                pltpu.SemaphoreType.DMA((pieces,)),
            ],
            compiler_params=pltpu.CompilerParams(
                collective_id=0, has_side_effects=True, vmem_limit_bytes=48 * 1024 * 1024
            ),
        )(*[pltpu.with_memory_space_constraint(a, pltpu.HBM) for a in operands])
        fgrad, gw_in, gb_in, gw_out = pl.pallas_call(
            unpack_kernel,
            out_shape=(
                jax.ShapeDtypeStruct((feat_width, trials), jnp.float32),
                jax.ShapeDtypeStruct((width, hidden_width), jnp.float32),
                jax.ShapeDtypeStruct((1, hidden_width), jnp.float32),
                jax.ShapeDtypeStruct((feat_width, hidden_width), jnp.float32),
            ),
            in_specs=[vmem] * 2,
            out_specs=(vmem,) * 4,
            compiler_params=pltpu.CompilerParams(vmem_limit_bytes=4 * 1024 * 1024),
        )(fgrad, sums)
        return fgrad, gw_in, gb_in[0], jnp.transpose(gw_out)

    split = ("groups", "rows", "cols")
    return jax.shard_map(
        body,
        mesh=mesh,
        in_specs=(
            P(None, split), P(split), P(), P(None, split), P(None, split), P(split), P(), P(), P(),
        ),
        out_specs=(P(None, split), P("groups", None), P("groups"), P("groups", None)),
        check_vma=False,
    )
```

```python
import functools
import math

import jax
import jax.numpy as jnp
from jax import lax
from jax.experimental import pallas as pl
from jax.experimental.pallas import tpu as pltpu
from jax.sharding import PartitionSpec as P

kernel_rate = 1.0
MESH = pl.DeviceIdType.MESH
LANES = 128


def split3(value):
    high = value.astype(jnp.bfloat16).astype(jnp.float32)
    rest = value - high
    mid = rest.astype(jnp.bfloat16).astype(jnp.float32)
    low = (rest - mid).astype(jnp.bfloat16).astype(jnp.float32)
    return high, mid, low


def whole_kernel(
    R, C,
    *refs_and_scratch,
):
    operands, refs = refs_and_scratch[:9], refs_and_scratch[9:]
    fgrad_ref, sums_ref, *refs = refs
    staged, (load_sem, *refs) = refs[:9], refs[9:]
    inputs_ref, ids_ref, table_ref, probes_ref, solves_ref, alpha_ref, w_in_ref, b_in_ref, w_out_t_ref = staged
    (
        buf, left_buf, swap, parts, rs_buf, ag_buf, ag_size,
        recv_sem, send_sem, core_send, core_recv, rs_send, rs_recv, ag_send, ag_recv,
    ) = refs
    n = R * C
    r, c = lax.axis_index("rows"), lax.axis_index("cols")
    me = r * C + c
    trials = inputs_ref.shape[1]
    feat_width = w_out_t_ref.shape[0]
    probe_count = probes_ref.shape[0]
    pieces = parts.shape[0]

    def coords(q):
        return {"rows": q // C, "cols": lax.rem(q, C)}

    def other(k):
        return me ^ (n - k)

    barrier = pltpu.get_barrier_semaphore()

    @pl.loop(1, n)
    def _(k):
        pl.semaphore_signal(barrier, inc=1, device_id=coords(other(k)), device_id_type=MESH)

    loads = [
        pltpu.make_async_copy(operands[k], staged[k], load_sem.at[k]) for k in range(9)
    ]
    for load in loads:
        load.start()

    for load in loads:
        load.wait()

    ids = ids_ref[...]
    lo, hi = lax.rem(ids, LANES), ids // LANES
    flat = table_ref[...]
    tasks = flat.shape[1]
    groups = -(-tasks // (8 * LANES)) * 8
    flat = jnp.concatenate([flat, jnp.zeros((1, groups * LANES - tasks), jnp.float32)], 1)
    table = jnp.concatenate([flat[:, k * LANES : (k + 1) * LANES] for k in range(groups)], 0)
    hot = (lax.broadcasted_iota(jnp.int32, (LANES, trials), 0) == lo).astype(jnp.float32).astype(jnp.bfloat16)
    terms = jnp.concatenate(split3(table), 0).astype(jnp.bfloat16)
    found = jnp.dot(terms, hot, preferred_element_type=jnp.float32)
    found = found[:groups] + found[groups : 2 * groups] + found[2 * groups :]
    mine = lax.broadcasted_iota(jnp.int32, (groups, trials), 0) == hi
    scale = jnp.sum(jnp.where(mine, found, 0.0), 0, keepdims=True)

    inputs = inputs_ref[...]
    width, half = inputs.shape[0], trials // 2
    raw_lanes = width + 2 * probe_count
    pad = -trials % LANES
    raw = jnp.concatenate(
        [
            inputs.astype(jnp.float32),
            solves_ref[...] * scale,
            probes_ref[...] * scale,
            jnp.broadcast_to(alpha_ref[...] * scale, (LANES - raw_lanes, trials)),
        ],
        0,
    )
    raw = jnp.transpose(jnp.concatenate([raw, jnp.zeros((LANES, pad), jnp.float32)], 1))[:trials]
    raw = raw.astype(jnp.bfloat16).astype(jnp.float32)

    chips = n // 2
    here, side = r * (C // 2) + c // 2, lax.rem(c, 2)
    main_part = jnp.concatenate([raw[:half, :raw_lanes], raw[half:, :raw_lanes]], 1)
    tile_lane = lax.broadcasted_iota(jnp.int32, (16, LANES), 1)
    a_part = jnp.zeros((16, LANES), jnp.float32)
    for k in range(trials // 16):
        a_part = jnp.where(tile_lane == k, raw[16 * k : 16 * k + 16, raw_lanes : raw_lanes + 1], a_part)
    buf[here, :half] = main_part.astype(jnp.bfloat16)
    buf[here, half:] = a_part.astype(jnp.bfloat16)

    pl.semaphore_wait(barrier, n - 1)

    def send(k):
        chip = here ^ k
        pltpu.make_async_remote_copy(
            src_ref=buf.at[here], dst_ref=buf.at[here], send_sem=send_sem, recv_sem=recv_sem.at[here],
            device_id={"rows": chip // (C // 2), "cols": lax.rem(chip, C // 2) * 2 + side},
            device_id_type=MESH,
        ).start()

    far = chips // 2

    @pl.loop(far, chips)
    def _(k):
        send(k)

    @pl.loop(1, far)
    def _(k):
        send(k)

    w_in, b_in = w_in_ref[...], b_in_ref[...]
    hidden_width = w_in.shape[1]
    preact = lax.dot_general(
        inputs, w_in, (((0,), (0,)), ((), ())), preferred_element_type=jnp.float32
    ) + b_in
    sig = 1.0 / (1.0 + jnp.exp(-preact))
    hidden = (preact * sig).astype(jnp.bfloat16)
    w_out_t = w_out_t_ref[...]
    feats = lax.dot_general(
        hidden, w_out_t, (((1,), (1,)), ((), ())), preferred_element_type=jnp.float32
    ).astype(jnp.bfloat16)
    feats_f = feats.astype(jnp.float32)
    sqnorm = jnp.sum(feats_f * feats_f, 1, keepdims=True)
    vecs = raw[:, width : width + LANES - feat_width]

    first_u, first_z = feat_width, feat_width + probe_count
    at_a = feat_width + 2 * probe_count
    lane = lax.broadcasted_iota(jnp.int32, (trials, LANES), 1)
    n_hi, n_mid, n_lo = split3(sqnorm)
    base = jnp.concatenate([feats_f, vecs], 1)
    rate = kernel_rate / feat_width
    row_exp = jnp.where(
        lane < feat_width,
        base * (2.0 * rate),
        jnp.where(
            lane <= at_a, 0.0,
            jnp.where(
                lane <= at_a + 3, -rate,
                jnp.where(
                    lane == at_a + 4, n_hi * -rate,
                    jnp.where(
                        lane == at_a + 5, n_mid * -rate,
                        jnp.where(lane == at_a + 6, n_lo * -rate, 0.0),
                    ),
                ),
            ),
        ),
    )
    swapped = jnp.concatenate(
        [feats_f, vecs[:, probe_count : 2 * probe_count], vecs[:, :probe_count], vecs[:, 2 * probe_count :]], 1
    )
    row_pair = jnp.where(
        lane < feat_width, 0.0,
        jnp.where(lane < at_a, swapped * (0.5 / probe_count), jnp.where(lane == at_a, -swapped, 0.0)),
    )
    left_buf[0, 0] = row_exp.astype(jnp.bfloat16)
    left_buf[0, 1] = row_pair.astype(jnp.bfloat16)

    def core_copy(refs, which):
        return pltpu.make_async_remote_copy(
            src_ref=refs.at[0], dst_ref=refs.at[1], send_sem=core_send.at[which], recv_sem=core_recv.at[which],
            device_id={"rows": r, "cols": c ^ 1}, device_id_type=MESH,
        )

    def wait_chip(k):
        chip = here ^ k
        pltpu.make_async_copy(buf.at[chip], buf.at[chip], recv_sem.at[chip]).wait()

    core_copy(left_buf, 0).start()
    core_copy(left_buf, 0).wait()
    left = jnp.concatenate([left_buf[0, 0], left_buf[1, 0], left_buf[0, 1], left_buf[1, 1]], 0)

    blank = jnp.zeros((width, hidden_width), jnp.bfloat16)
    gap = jnp.zeros((2 * probe_count, 2 * hidden_width), jnp.bfloat16)
    first_layer = jnp.concatenate(
        [
            jnp.concatenate([w_in, blank], 1),
            gap,
            jnp.concatenate([blank, w_in], 1),
            gap,
        ],
        0,
    )
    bias = jnp.concatenate([b_in, b_in], 1)
    second_layer = jnp.concatenate([w_out_t, jnp.zeros((LANES - feat_width, hidden_width), jnp.bfloat16)], 0)
    s_row = lax.broadcasted_iota(jnp.int32, (2 * LANES, LANES), 0)
    s_lane = lax.broadcasted_iota(jnp.int32, (2 * LANES, LANES), 1)
    lane2 = lax.broadcasted_iota(jnp.int32, (trials, LANES), 1)
    block = lax.rem(lax.broadcasted_iota(jnp.int32, (trials, LANES), 0), half) // 16
    places, a_masks = [], []
    for h in range(2):
        vec_place = (s_row == s_lane - feat_width + width + h * raw_lanes) & (s_lane >= feat_width) & (s_lane < at_a)
        place = vec_place | ((s_row >= LANES) & (s_lane == at_a))
        places.append(place.astype(jnp.float32).astype(jnp.bfloat16))
        a_masks.append((lane2 == block + h * (half // 16)).astype(jnp.float32).astype(jnp.bfloat16))

    def columns(pair):
        blocks = buf[pl.ds(2 * pair, 2)]
        main = blocks[:, :half].reshape(trials, LANES)
        tiles = jnp.concatenate([blocks[0, half:]] * (half // 16) + [blocks[1, half:]] * (half // 16), 0)
        pre = jnp.dot(main, first_layer, preferred_element_type=jnp.float32) + bias
        hid = (pre * (1.0 / (1.0 + jnp.exp(-pre)))).astype(jnp.bfloat16)
        found = []
        for h in range(2):
            value = lax.dot_general(
                hid[:, h * hidden_width : (h + 1) * hidden_width], second_layer,
                (((1,), (1,)), ((), ())), preferred_element_type=jnp.float32,
            ) + jnp.dot(
                jnp.concatenate([main, tiles * a_masks[h]], 1), places[h], preferred_element_type=jnp.float32
            )
            value = value.astype(jnp.bfloat16).astype(jnp.float32)
            norm = jnp.sum(jnp.where(lane2 < feat_width, value * value, 0.0), 1, keepdims=True)
            high, mid, low = split3(norm)
            found.append(
                jnp.where(
                    lane2 <= at_a, value,
                    jnp.where(
                        lane2 == at_a + 1, high,
                        jnp.where(
                            lane2 == at_a + 2, mid,
                            jnp.where(lane2 == at_a + 3, low, jnp.where(lane2 <= at_a + 6, 1.0, 0.0)),
                        ),
                    ),
                )
            )
        return jnp.concatenate(found, 0).astype(jnp.bfloat16)

    def add_columns(cols, total, sums):
        both = lax.dot_general(left, cols, (((1,), (1,)), ((), ())), preferred_element_type=jnp.float32)
        weight = both[2 * trials :] * jnp.exp(both[: 2 * trials])
        for j in range(2 * trials // LANES):
            sums = sums + weight[:, j * LANES : (j + 1) * LANES]
        total = total + jnp.dot(weight.astype(jnp.bfloat16), cols, preferred_element_type=jnp.float32)
        return total, sums

    def step(p, carry):
        cols, total, sums = carry
        wait_chip(2 * p)
        wait_chip(2 * p + 1)
        later = columns((here // 2) ^ p)
        return (later, *add_columns(cols, total, sums))

    empty = jnp.zeros((2 * trials, LANES), jnp.float32)
    wait_chip(1)
    carry = (columns(here // 2), empty, empty)
    carry = lax.fori_loop(1, chips // 2, step, carry, unroll=chips <= 8)
    total, sums = add_columns(*carry)

    def share(first):
        weight_sum = jnp.sum(sums[first : first + trials], 1, keepdims=True)
        return jnp.where(lane2 < feat_width, total[first : first + trials], weight_sum)

    swap[0] = share(trials)
    core_copy(swap, 1).start()
    mixed = share(0)
    core_copy(swap, 1).wait()
    mixed = mixed + swap[1]
    total, weight_sum = mixed[:, :feat_width], mixed[:, feat_width : feat_width + 1]
    feat_grad = (total - weight_sum * feats_f) * (2.0 * rate)
    grad_feats = feat_grad.astype(jnp.bfloat16)
    order = sorted(range(R), key=lambda k: abs(2 * k - R + 1))[:2]
    owners = len(order) * C
    rank = jnp.where(r == order[0], c, jnp.where(r == order[-1], (len(order) - 1) * C + c, owners))
    held = -(-pieces // owners)

    def owner(p):
        q = lax.rem(p, owners)
        return {"rows": jnp.where(q < C, order[0], order[-1]), "cols": lax.rem(q, C)}

    def piece_copy(p):
        return pltpu.make_async_remote_copy(
            src_ref=parts.at[p], dst_ref=rs_buf.at[p // owners, me], send_sem=rs_send.at[p],
            recv_sem=rs_recv.at[p // owners], device_id=owner(p), device_id_type=MESH,
        )

    def send_pieces(values, first):
        count = values.shape[0] // 8
        for p in range(count):
            for h in range(2):
                part = values[8 * p : 8 * p + 8, h * LANES : (h + 1) * LANES]
                parts[first + p, 8 * h : 8 * h + 8] = part.astype(parts.dtype)

        @pl.loop(first, first + count)
        def _(p):
            @pl.when(lax.rem(p, owners) != rank)
            def _():
                piece_copy(p).start()

    g_out = lax.dot_general(
        grad_feats, hidden, (((0,), (0,)), ((), ())), preferred_element_type=jnp.float32
    )
    send_pieces(g_out, 0)
    grad_hidden = jnp.dot(grad_feats, w_out_t, preferred_element_type=jnp.float32)
    grad_pre = grad_hidden * (sig * (1.0 + preact * (1.0 - sig)))
    g_in = jnp.dot(inputs, grad_pre.astype(jnp.bfloat16), preferred_element_type=jnp.float32)
    bias_terms = split3(jnp.sum(grad_pre, 0, keepdims=True))
    g_bias = jnp.concatenate([*bias_terms, jnp.zeros((5, hidden_width), jnp.float32)], 0)
    send_pieces(jnp.concatenate([g_in, g_bias], 0), feat_width // 8)

    wide = jnp.concatenate([feat_grad, jnp.zeros((trials, LANES - feat_width), jnp.float32)], 1)
    wide = jnp.concatenate([wide, jnp.zeros((pad, LANES), jnp.float32)], 0)
    fgrad_ref[...] = jnp.transpose(wide)[:feat_width, :trials]

    def ag_copy(p, k):
        return pltpu.make_async_remote_copy(
            src_ref=ag_buf.at[p], dst_ref=ag_buf.at[p], send_sem=ag_send.at[p // owners], recv_sem=ag_recv.at[p],
            device_id=coords(other(k)), device_id_type=MESH,
        )

    factor = 1.0 / math.sqrt(trials * n)
    for h in range(held):
        p = rank + h * owners

        @pl.when((rank < owners) & (p < pieces))
        def _():
            rs_buf[h, me] = parts[p]
            view = rs_buf.at[h, pl.ds(0, n - 1)]
            pltpu.make_async_copy(view, view, rs_recv.at[h]).wait()
            summed = jnp.sum(rs_buf[h].astype(jnp.float32), 0) * factor
            ag_buf[p] = summed.astype(jnp.bfloat16)

            @pl.loop(1, n)
            def _(k):
                ag_copy(p, k).start()

    @pl.loop(0, pieces)
    def _(p):
        @pl.when(lax.rem(p, owners) != rank)
        def _():
            pltpu.make_async_copy(ag_buf.at[p], ag_buf.at[p], ag_recv.at[p]).wait()

    sums_ref[...] = ag_buf[...]

    view = buf.at[pl.ds(0, chips - 1)]
    pltpu.make_async_copy(view, view, send_sem).wait()

    @pl.loop(0, pieces)
    def _(p):
        @pl.when(lax.rem(p, owners) != rank)
        def _():
            piece_copy(p).wait_send()

    for h in range(held):
        @pl.when((rank < owners) & (rank + h * owners < pieces))
        def _():
            pltpu.make_async_copy(ag_size, ag_size, ag_send.at[h]).wait()


def unpack_kernel(fgrad_ref, sums_ref, fgrad_out, gw_in_ref, gb_in_ref, gw_out_ref):
    def unpack(first, count):
        rows = []
        for p in range(first, first + count):
            piece = sums_ref[p].astype(jnp.float32)
            rows.append(jnp.concatenate([piece[:8], piece[8:]], 1))
        return jnp.concatenate(rows, 0) if count > 1 else rows[0]

    in_pieces, out_pieces = gw_in_ref.shape[0] // 8, gw_out_ref.shape[0] // 8
    fgrad_out[...] = fgrad_ref[...]
    gw_out_ref[...] = unpack(0, out_pieces)
    gw_in_ref[...] = unpack(out_pieces, in_pieces)
    gb_in_ref[...] = jnp.sum(unpack(in_pieces + out_pieces, 1), 0, keepdims=True)


def solution(mesh):
    R, C = mesh.shape["rows"], mesh.shape["cols"]
    n = R * C

    def body(inputs, task_ids, scale_table, probes, solves, alpha_solve, w_in, b_in, w_out):
        width, trials = inputs.shape
        hidden_width, feat_width = w_out.shape
        pieces = (width + feat_width) // 8 + 1
        operands = (
            inputs, task_ids[None, :], scale_table[None, :], probes, solves, alpha_solve[None, :], w_in, b_in[None, :],
            w_out.T,
        )
        staged = [pltpu.VMEM(a.shape, a.dtype) for a in operands]
        held = -(-pieces // (min(R, 2) * C))
        vmem = pl.BlockSpec(memory_space=pltpu.VMEM)
        fgrad, sums = pl.pallas_call(
            functools.partial(whole_kernel, R, C),
            out_shape=(
                jax.ShapeDtypeStruct((feat_width, trials), jnp.float32),
                jax.ShapeDtypeStruct((pieces, 16, LANES), jnp.bfloat16),
            ),
            in_specs=[pl.BlockSpec(memory_space=pltpu.HBM)] * 9,
            out_specs=(vmem,) * 2,
            scratch_shapes=staged
            + [
                pltpu.SemaphoreType.DMA((9,)),
                pltpu.VMEM((n // 2, trials // 2 + 16, LANES), jnp.bfloat16),
                pltpu.VMEM((2, 2, trials, LANES), jnp.bfloat16),
                pltpu.VMEM((2, trials, LANES), jnp.float32),
                pltpu.VMEM((pieces, 16, LANES), jnp.bfloat16),
                pltpu.VMEM((held, n, 16, LANES), jnp.bfloat16),
                pltpu.VMEM((pieces, 16, LANES), jnp.bfloat16),
                pltpu.VMEM((n - 1, 16, LANES), jnp.bfloat16),
                pltpu.SemaphoreType.DMA((n // 2,)),
                pltpu.SemaphoreType.DMA,
                pltpu.SemaphoreType.DMA((2,)),
                pltpu.SemaphoreType.DMA((2,)),
                pltpu.SemaphoreType.DMA((pieces,)),
                pltpu.SemaphoreType.DMA((held,)),
                pltpu.SemaphoreType.DMA((held,)),
                pltpu.SemaphoreType.DMA((pieces,)),
            ],
            compiler_params=pltpu.CompilerParams(
                collective_id=0, has_side_effects=True, vmem_limit_bytes=48 * 1024 * 1024
            ),
        )(*[pltpu.with_memory_space_constraint(a, pltpu.HBM) for a in operands])
        fgrad, gw_in, gb_in, gw_out = pl.pallas_call(
            unpack_kernel,
            out_shape=(
                jax.ShapeDtypeStruct((feat_width, trials), jnp.float32),
                jax.ShapeDtypeStruct((width, hidden_width), jnp.float32),
                jax.ShapeDtypeStruct((1, hidden_width), jnp.float32),
                jax.ShapeDtypeStruct((feat_width, hidden_width), jnp.float32),
            ),
            in_specs=[vmem] * 2,
            out_specs=(vmem,) * 4,
            compiler_params=pltpu.CompilerParams(vmem_limit_bytes=4 * 1024 * 1024),
        )(fgrad, sums)
        return fgrad, gw_in, gb_in[0], jnp.transpose(gw_out)

    split = ("groups", "rows", "cols")
    return jax.shard_map(
        body,
        mesh=mesh,
        in_specs=(
            P(None, split), P(split), P(), P(None, split), P(None, split), P(split), P(), P(), P(),
        ),
        out_specs=(P(None, split), P("groups", None), P("groups"), P("groups", None)),
        check_vma=False,
    )
```
